32 devices in a mesh: blk: 16 (over z, y, core), shard: 2 (over x).
Axes of the slice: x: 2, y: 2, z: 4, core: 2. Of those that a mesh axis runs over, the one named last changes fastest.
Arguments:
- queries: bfloat16 [4096, 1536], P(('blk', 'shard')), may hold values from -16 to 16
- passages: bfloat16 [256, 1536], P(('blk', 'shard')), may hold values from -18 to 18
- neg_pool: bfloat16 [32768, 1536], P(('blk', 'shard')), may hold values from -18 to 18
- hard_ids: int32 [4096, 7], P(('blk', 'shard')), may hold values from 0 to 2047, as said below
- positives: int32 [4096], P(('blk', 'shard')), may hold values from 0 to 255
Outputs:
- query_grad: float32 [4096, 1536], P(('blk', 'shard'))
- passage_grad: float32 [256, 1536], P(('blk', 'shard'))
- pool_grad: float32 [32768, 1536], P(('blk', 'shard'))
The draws below stay inside these ranges and needn't reach their ends.
Inputs may be any that keep to these rules, and one draw needn't show every extreme that they name: `hard_ids`: entry v names the pool row of the query's own blk index held by the shard index v // 1024. Among the 896 ids of one device's queries at most 597 fall on any one shard index; for every blk index one shard index receives exactly 597 ids from each of the 2 devices of that blk index.
All inputs are finite; a program needn't handle non-finite values.
Results may differ from the reference program's by a relative error of at most 0.0038.
Values may be sent and summed in bfloat16 or wider, within the bound.
No kernel may reach another device: no remote copies, remote signals or barrier semaphores. Data moves between devices by JAX's collectives and lax.ppermute only.
A program may use at most 128 MiB of HBM per device.

```python
import jax
import jax.numpy as jnp
from jax import lax

D = 1536
Q_DEV = 128
POOL_DEV = 1024
NEG_K = 7
QUERIES = 4096
PASSAGES = 256
POOL = 32768
CAP = 597
N_BLK = 16
N_SHARD = 2


def log_spread(key, count, low, high):
    return jnp.exp(jax.random.uniform(key, (count,), jnp.float32, jnp.log(low), jnp.log(high)))


def draw_passages(key, part):
    key = jax.random.fold_in(key, 5)
    key_scale, key_noise = jax.random.split(key, 2)
    drawn_rows = jnp.clip(jax.random.normal(key_noise, (PASSAGES, D), jnp.float32), -6.0, 6.0)
    return (drawn_rows * log_spread(key_scale, PASSAGES, 0.3, 3.0)[:, None]).astype(jnp.bfloat16)


def draw_queries(key, part):
    key = jax.random.fold_in(key, 7)
    key_scale, key_rows = jax.random.split(key, 2)
    row_scales = log_spread(key_scale, QUERIES, 0.5, 2.0)
    drawn_rows = jnp.clip(jax.random.normal(key_rows, (QUERIES, D), jnp.float32), -6.0, 6.0)
    return (drawn_rows * row_scales[:, None]).astype(jnp.bfloat16)


def draw_hard_ids(key, part):
    key = jax.random.fold_in(key, 11)
    key_busy, key_share, key_order, key_row = jax.random.split(key, 4)
    device_count = N_BLK * N_SHARD
    requests = Q_DEV * NEG_K
    busy_group = jax.random.randint(key_busy, (N_BLK,), 0, N_SHARD)
    busy_owner = jnp.repeat(busy_group, N_SHARD)
    owner_iota = jnp.arange(N_SHARD, dtype=jnp.int32)
    is_busy = owner_iota[None, :] == busy_owner[:, None]
    share_w = jnp.where(is_busy, 0, jax.random.randint(key_share, (device_count, N_SHARD), 80, 121))
    spare_total = requests - CAP
    counts = spare_total * share_w // jnp.sum(share_w, axis=1, keepdims=True)
    shortfall = spare_total - jnp.sum(counts, axis=1)
    free_rank = owner_iota[None, :] - (owner_iota[None, :] > busy_owner[:, None]).astype(jnp.int32)
    counts = counts + jnp.where(jnp.logical_and(~is_busy, free_rank < shortfall[:, None]), 1, 0)
    counts = jnp.where(is_busy, CAP, counts)
    count_ends = jnp.cumsum(counts, axis=1)
    slot_index = jnp.arange(requests, dtype=jnp.int32)
    owner_of = jnp.sum((slot_index[None, :, None] >= count_ends[:, None, :]).astype(jnp.int32), axis=2)
    order_keys = jax.random.split(key_order, device_count)
    owner_of = jax.vmap(lambda k_one, line: jax.random.permutation(k_one, line))(order_keys, owner_of)
    row_pick = jax.random.randint(key_row, (device_count, requests), 0, POOL_DEV)
    flat_ids = owner_of * POOL_DEV + row_pick
    return flat_ids.reshape(device_count * Q_DEV, NEG_K).astype(jnp.int32)


def set_ends(result, key, smallest, largest):
    dims = result.shape
    place = [jax.random.randint(jax.random.fold_in(key, axis), (), 0, dims[axis]) for axis in range(len(dims))]
    result = result.at[tuple(place)].set(smallest)
    longest = dims.index(max(dims))
    place[longest] = (place[longest] + 1) % dims[longest]
    return result.at[tuple(place)].set(largest)


def block_levels(rng, shape, shards, smallest, largest):
    def one(axis_at, parts):
        draws = jax.random.uniform(jax.random.fold_in(jax.random.fold_in(rng, 6), axis_at), (parts,), jnp.float32, smallest / len(shards), largest / len(shards))
        return jnp.repeat(jnp.exp(draws), shape[axis_at] // parts).reshape((-1,) + (1,) * (len(shape) - axis_at - 1))

    gain = one(*shards[0])
    for cut in shards[1:]:
        gain = gain * one(*cut)
    return gain


def centred(key, shape, width, reach, cuts=(), kind=jnp.bfloat16):
    drawn = jax.random.normal(key, shape, jnp.float32) * width
    if len(cuts) > 0:
        drawn = block_levels(key, shape, cuts, -0.22, 0.18) * drawn
    return jnp.clip(drawn, min=-reach, max=reach).astype(kind)


def setup_inputs(seed: int = 0) -> dict:
    key_list = jax.random.split(jax.random.key(seed), 6)
    return {
        "queries": draw_queries(jax.random.fold_in(key_list[5], 71), 0),
        "passages": draw_passages(jax.random.fold_in(key_list[5], 71), 0),
        "neg_pool": centred(key_list[2], (POOL, D), 3.0, 18.0, ((0, 32),)),
        "hard_ids": draw_hard_ids(jax.random.fold_in(key_list[5], 71), 0),
        "positives": set_ends(jax.random.randint(key_list[4], (QUERIES,), 0, PASSAGES), jax.random.fold_in(key_list[4], 1), 0, PASSAGES - 1).astype(jnp.int32),
    }


def reference(queries, passages, neg_pool, hard_ids, positives):
    scaling = D ** -0.5
    group_rows = Q_DEV * N_SHARD
    pool_rows = POOL_DEV * N_SHARD
    passage_ids = jnp.arange(PASSAGES, dtype=jnp.int32)

    def per_group(grad_acc, item):
        group_q, group_ids, group_pos, group_pool = item
        negatives = jnp.take(group_pool, group_ids.reshape(-1), axis=0).reshape(group_rows, NEG_K, D)
        scores = jnp.dot(group_q, passages.T, preferred_element_type=jnp.float32) * scaling
        hard_scores = jnp.einsum("qd,qkd->qk", group_q.astype(jnp.float32), negatives.astype(jnp.float32)) * scaling
        row_max = jnp.maximum(jnp.max(scores, axis=1), jnp.max(hard_scores, axis=1))
        exp_total = jnp.sum(jnp.exp(scores - row_max[:, None]), axis=1) + jnp.sum(jnp.exp(hard_scores - row_max[:, None]), axis=1)
        log_total = row_max + jnp.log(exp_total)
        hit = (group_pos[:, None] == passage_ids[None, :]).astype(jnp.float32)
        weights_bf = (jnp.exp(scores - log_total[:, None]) - hit).astype(jnp.bfloat16)
        hard_weights = jnp.exp(hard_scores - log_total[:, None]).astype(jnp.bfloat16)
        hard_weights = lax.optimization_barrier(hard_weights)
        hard_part = jnp.einsum("qk,qkd->qd", hard_weights.astype(jnp.float32), negatives.astype(jnp.float32))
        q_grad = (jnp.dot(weights_bf, passages, preferred_element_type=jnp.float32) + hard_part) * scaling
        grad_acc = grad_acc + jnp.dot(weights_bf.T, group_q, preferred_element_type=jnp.float32)
        slot_terms = (hard_weights.astype(jnp.float32)[:, :, None] * group_q.astype(jnp.float32)[:, None, :]).astype(jnp.bfloat16)
        slot_terms = lax.optimization_barrier(slot_terms)
        own_grad = jax.ops.segment_sum(slot_terms.reshape(-1, D).astype(jnp.float32), group_ids.reshape(-1).astype(jnp.int32), num_segments=pool_rows) * scaling
        return grad_acc, (q_grad, own_grad)

    inputs = (queries.reshape(N_BLK, group_rows, D), hard_ids.reshape(N_BLK, group_rows, NEG_K),
              positives.reshape(N_BLK, group_rows), neg_pool.reshape(N_BLK, pool_rows, D))
    grad_acc, (q_grads, pool_grads) = lax.scan(per_group, jnp.zeros((PASSAGES, D), jnp.float32), inputs)
    return q_grads.reshape(QUERIES, D), grad_acc * scaling, pool_grads.reshape(POOL, D)
```

```python
import jax
import jax.numpy as jnp
from jax import lax
from jax.sharding import PartitionSpec as P


def bit_order(count):
    bits = [1 << t for t in range(count.bit_length() - 1)]
    return bits[2:] + bits[:2][::-1]


def across(x, axis, count, distance):
    return lax.ppermute(x, axis, [(i, i ^ distance) for i in range(count)])


def shifted(x, axis, count, distance):
    return lax.ppermute(x, axis, [((i + distance) % count, i) for i in range(count)])


def body(queries, passages, neg_pool, hard_ids, positives):
    rows, features = queries.shape
    neg_count = hard_ids.shape[1]
    tile = passages.shape[0]
    pool_rows = neg_pool.shape[0]
    scaling = features ** (-0.5)
    owners = lax.axis_size("shard")
    blocks = lax.axis_size("blk")
    my_shard = lax.axis_index("shard")
    my_blk = lax.axis_index("blk")

    marks = jnp.concatenate([hard_ids, positives[:, None]], axis=1)
    group_marks = jnp.concatenate(
        [marks] + [shifted(marks, "shard", owners, d) for d in range(1, owners)], axis=0
    )
    group_q = jnp.concatenate(
        [queries] + [shifted(queries, "shard", owners, d) for d in range(1, owners)], axis=0
    )

    order = bit_order(blocks)
    keys = passages
    key_blk = jnp.zeros((1,), jnp.int32)
    for bit in order:
        keys = jnp.concatenate([keys, across(keys, "blk", blocks, bit)], axis=0)
        key_blk = jnp.concatenate([key_blk, key_blk ^ bit], axis=0)
    key_ids = (
        ((key_blk ^ my_blk) * owners + my_shard)[:, None] * tile
        + jnp.arange(tile, dtype=jnp.int32)[None, :]
    ).reshape(-1)

    def dots(a, b):
        return lax.dot_general(a, b, (((1,), (1,)), ((), ())), preferred_element_type=jnp.float32)

    local_ids = group_marks[:, :neg_count] - my_shard * pool_rows
    slots = jnp.arange(pool_rows, dtype=jnp.int32)[None, :]
    times = sum((local_ids[:, k : k + 1] == slots).astype(jnp.float32) for k in range(neg_count))
    hard = jnp.where(times > 0, dots(group_q, neg_pool) * scaling, -jnp.inf)
    score = dots(group_q, keys) * scaling
    part_max = jnp.maximum(jnp.max(hard, axis=1), jnp.max(score, axis=1))
    part_sum = jnp.sum(times * jnp.exp(hard - part_max[:, None]), axis=1) + jnp.sum(
        jnp.exp(score - part_max[:, None]), axis=1
    )
    part = jnp.stack([part_max, part_sum])
    if owners == 2:
        other = shifted(part, "shard", owners, 1)
        parts = jnp.stack([part, jnp.roll(other, rows, axis=1)])
    else:
        whole = lax.all_gather(jnp.roll(part, my_shard * rows, axis=1), "shard", axis=0)
        parts = jnp.roll(whole, -my_shard * rows, axis=2)
    row_max = jnp.max(parts[:, 0], axis=0)
    log_total = row_max + jnp.log(
        jnp.sum(parts[:, 1] * jnp.exp(parts[:, 0] - row_max[None, :]), axis=0)
    )

    hit = (group_marks[:, neg_count:] == key_ids[None, :]).astype(jnp.float32)
    weights = (jnp.exp(score - log_total[:, None]) - hit).astype(jnp.bfloat16)
    hard_weights = jnp.exp(hard - log_total[:, None]).astype(jnp.bfloat16)
    hard_weights = (times * hard_weights.astype(jnp.float32)).astype(jnp.bfloat16)

    def spread(w, q):
        return lax.dot_general(w, q, (((0,), (0,)), ((), ())), preferred_element_type=jnp.float32)

    passage_acc = spread(weights, group_q) * scaling
    for bit in order[::-1]:
        half = passage_acc.shape[0] // 2
        sent = across(passage_acc[half:].astype(jnp.bfloat16), "blk", blocks, bit)
        passage_acc = passage_acc[:half] + sent.astype(jnp.float32)

    def query_part(d):
        piece = slice(d * rows, (d + 1) * rows)
        return (
            jnp.dot(weights[piece], keys, preferred_element_type=jnp.float32)
            + jnp.dot(hard_weights[piece], neg_pool, preferred_element_type=jnp.float32)
        ) * scaling

    back = [
        shifted(query_part(d).astype(jnp.bfloat16), "shard", owners, owners - d)
        for d in range(1, owners)
    ]
    query_grad = query_part(0) + sum(b.astype(jnp.float32) for b in back)
    pool_grad = spread(hard_weights, group_q) * scaling
    return query_grad, passage_acc, pool_grad


def solution(mesh):
    both = P(("blk", "shard"), None)
    in_specs = (both, both, both, both, P(("blk", "shard")))
    return jax.shard_map(
        body, mesh=mesh, in_specs=in_specs, out_specs=(both, both, both), check_vma=False
    )
```

```python
import functools

import jax
import jax.numpy as jnp
from jax import lax
from jax.experimental import pallas as pl
from jax.experimental.pallas import tpu as pltpu
from jax.sharding import PartitionSpec as P

VMEM = pl.BlockSpec(memory_space=pltpu.VMEM)
ANY = pl.BlockSpec(memory_space=pl.ANY)
HBM = pl.BlockSpec(memory_space=pltpu.HBM)
PARAMS = pltpu.CompilerParams(vmem_limit_bytes=40 * 2**20)
F32, BF16 = jnp.float32, jnp.bfloat16


def cost(micros):
    return pl.CostEstimate(flops=0, bytes_accessed=int(micros * 3.69e6), transcendentals=0)


NONE = -1e30


def across(x, axis, count, distance):
    return lax.ppermute(x, axis, [(i, i ^ distance) for i in range(count)])


def shifted(x, axis, count, distance):
    return lax.ppermute(x, axis, [((i + distance) % count, i) for i in range(count)])


def after(x, *others):
    return lax.optimization_barrier((x, *others))


def dot(a, b, over):
    return lax.dot_general(a, b, (over, ((), ())), preferred_element_type=F32)


ROWS_ROWS = ((1,), (1,))
ROWS_COLS = ((1,), (0,))
COLS_COLS = ((0,), (0,))


def count_ids(chunk, ids, times_ref):
    pool_rows, rows = times_ref.shape
    ids = ids - lax.axis_index("shard") * pool_rows
    for c in range(0, pool_rows, chunk):
        slot = lax.broadcasted_iota(jnp.int32, (chunk, rows), 0) + c
        times = jnp.zeros((chunk, rows), F32)
        for k in range(ids.shape[0]):
            times = times + jnp.where(slot == ids[k : k + 1, :], 1.0, 0.0)
        times_ref[c : c + chunk, :] = times


def scores_of(chunk, scaling, q_ref, pool_ref, hard_ref, times_ref, stat_ref, ready):
    pool_rows, rows = hard_ref.shape
    top = jnp.full((1, rows), NONE, F32)
    for c in range(0, pool_rows, chunk):
        ready(c)
        score = dot(pool_ref[c : c + chunk, :], q_ref[...], ROWS_ROWS) * scaling
        score = jnp.where(times_ref[c : c + chunk, :] > 0, score, NONE)
        hard_ref[c : c + chunk, :] = score
        top = jnp.maximum(top, jnp.max(score, axis=0, keepdims=True))
    total = jnp.zeros((1, rows), F32)
    for c in range(0, pool_rows, chunk):
        part = times_ref[c : c + chunk, :] * jnp.exp(hard_ref[c : c + chunk, :] - top)
        total = total + jnp.sum(part, axis=0, keepdims=True)
    stat_ref[0:1, :] = top
    stat_ref[1:2, :] = total


def own_kernel(
    chunk, scaling, ids_ref, pos_ref, tile_ref, q_ref, pool_ref,
    tile_here, all_q_ref, pool_here, marks_ref, hard_ref, times_ref, stat_ref, sems,
):
    rows = q_ref.shape[0]
    neg_count = ids_ref.shape[0]
    half = pool_ref.shape[0] // 2
    marks = [
        pltpu.make_async_copy(ids_ref, marks_ref.at[0:neg_count, :], sems.at[0]),
        pltpu.make_async_copy(pos_ref, marks_ref.at[neg_count : neg_count + 1, :], sems.at[1]),
    ]
    others = [
        pltpu.make_async_copy(q_ref, all_q_ref.at[0:rows, :], sems.at[2]),
        pltpu.make_async_copy(tile_ref, tile_here, sems.at[3]),
    ]
    halves = [
        pltpu.make_async_copy(
            pool_ref.at[c : c + half, :], pool_here.at[c : c + half, :], sems.at[4 + c // half]
        )
        for c in (0, half)
    ]
    for copy in marks + others + halves:
        copy.start()
    for copy in marks:
        copy.wait()
    count_ids(chunk, marks_ref[0:neg_count, :], times_ref)
    for copy in others:
        copy.wait()

    def ready(c):
        if c % half == 0:
            halves[c // half].wait()

    scores_of(
        chunk, scaling, all_q_ref.at[0:rows, :], pool_here, hard_ref, times_ref, stat_ref, ready
    )


def hard_shapes(pool_rows, rows):
    return [
        pltpu.VMEM((pool_rows, rows), F32),
        pltpu.VMEM((pool_rows, rows), F32),
        pltpu.VMEM((2, rows), F32),
    ]


def own_scores(pieces, ids, pos, tile, q, pool):
    rows, features = q.shape
    pool_rows = pool.shape[0]
    chunk = min(pool_rows, 128)
    return pl.pallas_call(
        functools.partial(own_kernel, chunk, features ** (-0.5)),
        in_specs=[HBM] * 5,
        out_specs=[VMEM] * 7,
        out_shape=[
            pltpu.VMEM(tile.shape, BF16),
            pltpu.VMEM((pieces * rows, features), BF16),
            pltpu.VMEM((pool_rows, features), BF16),
            pltpu.VMEM((ids.shape[0] + 1, rows), jnp.int32),
        ]
        + hard_shapes(pool_rows, rows),
        scratch_shapes=[pltpu.SemaphoreType.DMA((6,))],
        compiler_params=PARAMS,
        cost_estimate=cost(20),
        name="own_scores",
    )(*(pltpu.with_memory_space_constraint(x, pltpu.HBM) for x in (ids, pos, tile, q, pool)))


def group_kernel(piece, chunk, scaling, marks_ref, q_ref, pool_ref, _, all_q_ref, hard_ref, times_ref, stat_ref):
    rows = q_ref.shape[0]
    all_q_ref[piece * rows : (piece + 1) * rows, :] = q_ref[...]
    count_ids(chunk, marks_ref[0 : marks_ref.shape[0] - 1, :], times_ref)
    scores_of(
        chunk, scaling, q_ref, pool_ref, hard_ref, times_ref, stat_ref, lambda c: None
    )


def group_scores(piece, marks, q, pool, all_q):
    rows, features = q.shape
    pool_rows = pool.shape[0]
    return pl.pallas_call(
        functools.partial(group_kernel, piece, min(pool_rows, 128), features ** (-0.5)),
        in_specs=[VMEM] * 3 + [ANY],
        out_specs=[VMEM] * 4,
        out_shape=[jax.ShapeDtypeStruct(all_q.shape, BF16)] + hard_shapes(pool_rows, rows),
        input_output_aliases={3: 0},
        compiler_params=PARAMS,
        cost_estimate=cost(20),
        name="group_scores",
    )(marks, q, pool, all_q)


def score_kernel(scaling, keys_ref, q_ref, *refs):
    score_ref, part_ref = refs[-2:]
    stats = [r[...] for r in refs[:-2]]
    score = dot(keys_ref[...], q_ref[...], ROWS_ROWS) * scaling
    score_ref[...] = score
    stat = jnp.concatenate(stats, axis=1)
    hard_top, hard_sum = stat[0:1, :], stat[1:2, :]
    top = jnp.maximum(hard_top, jnp.max(score, axis=0, keepdims=True))
    part_ref[0:1, :] = top
    part_ref[1:2, :] = hard_sum * jnp.exp(hard_top - top) + jnp.sum(
        jnp.exp(score - top), axis=0, keepdims=True
    )


def passage_scores(keys, all_q, stats):
    held, group = keys.shape[0], all_q.shape[0]
    return pl.pallas_call(
        functools.partial(score_kernel, keys.shape[1] ** (-0.5)),
        in_specs=[VMEM] * (2 + len(stats)),
        out_specs=[VMEM] * 2,
        out_shape=[
            jax.ShapeDtypeStruct((held, group), F32),
            jax.ShapeDtypeStruct((2, group), F32),
        ],
        compiler_params=PARAMS,
        name="passage_scores",
    )(keys, all_q, *stats)


def weight_kernel(far, tile, owners, scaling, score_ref, q_ref, part_ref, other_ref, *refs):
    w_ref, log_ref, keep_ref, send_ref = refs[-4:]
    pos = jnp.concatenate([r[r.shape[0] - 1 :, :] for r in refs[:-4]], axis=1)
    held, group = score_ref.shape
    rows = group // owners
    if owners == 2:
        other = other_ref[...]
        parts = [
            part_ref[...],
            jnp.concatenate([other[:, rows:], other[:, :rows]], axis=1),
        ]
    else:
        parts = [other_ref[d] for d in range(owners)]
    top = functools.reduce(jnp.maximum, [p[0:1, :] for p in parts])
    total = sum(p[1:2, :] * jnp.exp(p[0:1, :] - top) for p in parts)
    log_total = top + jnp.log(total)
    log_ref[...] = log_total
    line = lax.broadcasted_iota(jnp.int32, (held, 1), 0)
    place = line // tile
    key_blk = (place % far) * 4 + ((place // far) % 2) * 2 + place // (2 * far)
    key_blk = key_blk ^ lax.axis_index("blk")
    key_id = (key_blk * owners + lax.axis_index("shard")) * tile + line % tile
    hit = jnp.where(key_id == pos, 1.0, 0.0)
    w = (jnp.exp(score_ref[...] - log_total) - hit).astype(BF16)
    w_ref[...] = w
    half = held // 2
    keep_ref[...] = dot(w[:half], q_ref[...], ROWS_COLS) * scaling
    send_ref[...] = (dot(w[half:], q_ref[...], ROWS_COLS) * scaling).astype(BF16)


def passage_weights(far, tile, owners, score, all_q, part, other, pos):
    held, group = score.shape
    features = all_q.shape[1]
    return pl.pallas_call(
        functools.partial(weight_kernel, far, tile, owners, features ** (-0.5)),
        in_specs=[VMEM] * (4 + len(pos)),
        out_specs=[VMEM] * 4,
        out_shape=[
            jax.ShapeDtypeStruct((held, group), BF16),
            jax.ShapeDtypeStruct((1, group), F32),
            jax.ShapeDtypeStruct((held // 2, features), F32),
            jax.ShapeDtypeStruct((held // 2, features), BF16),
        ],
        compiler_params=PARAMS,
        name="passage_weights",
    )(score, all_q, part, other, *pos)


def query_kernel(piece, scaling, hard_ref, times_ref, log_ref, w_ref, keys_ref, pool_ref, grad_ref, hw_ref):
    rows = hard_ref.shape[1]
    here = slice(piece * rows, (piece + 1) * rows)
    w = jnp.exp(hard_ref[...] - log_ref[:, here]).astype(BF16).astype(F32)
    hw = (times_ref[...] * w).astype(BF16)
    hw_ref[...] = hw
    grad = dot(hw, pool_ref[...], COLS_COLS) + dot(w_ref[:, here], keys_ref[...], COLS_COLS)
    grad_ref[...] = (grad * scaling).astype(grad_ref.dtype)


def query_part(piece, hard, times, log_total, w, keys, pool, dtype, micros=10):
    pool_rows, rows = hard.shape
    features = pool.shape[1]
    return pl.pallas_call(
        functools.partial(query_kernel, piece, features ** (-0.5)),
        in_specs=[VMEM] * 6,
        out_specs=[VMEM] * 2,
        out_shape=[
            jax.ShapeDtypeStruct((rows, features), dtype),
            jax.ShapeDtypeStruct((pool_rows, rows), BF16),
        ],
        compiler_params=PARAMS,
        cost_estimate=cost(micros),
        name="query_part",
    )(hard, times, log_total, w, keys, pool)


def pool_kernel(first, chunk, scaling, owners, q_ref, *refs):
    weights, (out_ref, buffer, sems) = refs[:owners], refs[-3:]
    copies = []
    for c in range(0, buffer.shape[0], chunk):
        w = jnp.concatenate([r[first + c : first + c + chunk, :] for r in weights], axis=1)
        buffer[c : c + chunk, :] = dot(w, q_ref[...], ROWS_COLS) * scaling
        copy = pltpu.make_async_copy(
            buffer.at[c : c + chunk, :],
            out_ref.at[first + c : first + c + chunk, :],
            sems.at[c // chunk],
        )
        copy.start()
        copies.append(copy)
    for copy in copies:
        copy.wait()


def pool_rows_grad(first, count, all_q, weights, so_far, micros):
    pool_rows = weights[0].shape[0]
    features = all_q.shape[1]
    chunk = min(count, 128)
    earlier = [] if so_far is None else [so_far]
    return pl.pallas_call(
        functools.partial(pool_kernel, first, chunk, features ** (-0.5), len(weights)),
        in_specs=[VMEM] * (1 + len(weights)) + [ANY] * len(earlier),
        out_specs=ANY,
        out_shape=jax.ShapeDtypeStruct((pool_rows, features), F32),
        scratch_shapes=[
            pltpu.VMEM((count, features), F32),
            pltpu.SemaphoreType.DMA((count // chunk,)),
        ],
        input_output_aliases={1 + len(weights): 0} if earlier else {},
        compiler_params=PARAMS,
        cost_estimate=cost(micros),
        name="pool_grad",
    )(all_q, *weights, *earlier)


def sum_kernel(chunk, *refs):
    terms, (out_ref, buffer, sems) = refs[:-3], refs[-3:]
    copies = []
    for c in range(0, buffer.shape[0], chunk):
        here = slice(c, c + chunk)
        buffer[here, :] = functools.reduce(jnp.add, [t[here, :].astype(F32) for t in terms])
        copy = pltpu.make_async_copy(
            buffer.at[here, :], out_ref.at[here, :], sems.at[c // chunk]
        )
        copy.start()
        copies.append(copy)
    for copy in copies:
        copy.wait()


def sum_terms(terms):
    rows = terms[0].shape[0]
    chunk = min(rows, 32)
    return pl.pallas_call(
        functools.partial(sum_kernel, chunk),
        in_specs=[VMEM] * len(terms),
        out_specs=ANY,
        out_shape=jax.ShapeDtypeStruct(terms[0].shape, F32),
        scratch_shapes=[
            pltpu.VMEM(terms[0].shape, F32),
            pltpu.SemaphoreType.DMA((rows // chunk,)),
        ],
        compiler_params=PARAMS,
        cost_estimate=cost(20),
        name="query_grad",
    )(*terms)


def body(queries, passages, neg_pool, hard_ids, positives):
    rows = queries.shape[0]
    tile = passages.shape[0]
    owners = lax.axis_size("shard")
    blocks = lax.axis_size("blk")
    my_shard = lax.axis_index("shard")

    group_q = [shifted(queries, "shard", owners, d) for d in range(1, owners)]
    my_tile, all_q, pool, marks, *found = own_scores(
        owners, hard_ids.T, positives.reshape(1, rows), passages, queries, neg_pool
    )
    group_marks = [marks] + [shifted(marks, "shard", owners, d) for d in range(1, owners)]
    hard = [found]
    for d in range(1, owners):
        all_q, *found = group_scores(d, group_marks[d], group_q[d - 1], pool, all_q)
        hard.append(found)

    far = blocks // 4
    keys = jnp.concatenate([my_tile] + [across(passages, "blk", blocks, 4 * z) for z in range(1, far)], axis=0)
    keys = lax.optimization_barrier(keys)
    for bit in (2, 1):
        if bit == 1:
            keys, hard, all_q = after(keys, hard, all_q)
        keys = lax.optimization_barrier(
            jnp.concatenate([keys, across(keys, "blk", blocks, bit)], axis=0)
        )

    score, part = passage_scores(keys, all_q, [h[2] for h in hard])
    if owners == 2:
        other = shifted(part, "shard", owners, 1)
    else:
        other = lax.all_gather(jnp.roll(part, my_shard * rows, axis=1), "shard", axis=0)
        other = jnp.roll(other, -my_shard * rows, axis=2)
    w, log_total, keep, send = passage_weights(
        far, tile, owners, score, all_q, part, other, group_marks
    )

    for step, bit in enumerate((1, 2)):
        got = across(send, "blk", blocks, bit).astype(F32)
        passage_grad = keep + got
        half = passage_grad.shape[0] // 2
        keep, send = passage_grad[:half], passage_grad[half:].astype(BF16)
        if step == 0:
            made = [
                query_part(d, hard[d][0], hard[d][1], log_total, w, keys, pool, BF16)
                for d in range(1, owners)
            ]
            own, own_w = query_part(0, hard[0][0], hard[0][1], log_total, w, keys, pool, F32)
            keep, send, made, own = after(keep, send, made, own)
            back = [
                shifted(grad, "shard", owners, owners - d) for d, (grad, _) in enumerate(made, 1)
            ]
            hard_w = [own_w] + [hw for _, hw in made]
    sent = passage_grad[tile:].astype(BF16)
    far_terms = [
        across(sent[(z - 1) * tile : z * tile], "blk", blocks, 4 * z) for z in range(1, far)
    ]
    pool_grad = pool_rows_grad(0, neg_pool.shape[0], all_q, hard_w, None, 20)
    query_grad = sum_terms([own] + back)
    passage_grad, pool_grad, query_grad = after(passage_grad, pool_grad, query_grad)
    passage_grad = passage_grad[:tile] + sum(t.astype(F32) for t in far_terms)

    return query_grad, passage_grad, pool_grad


def solution(mesh):
    both = P(("blk", "shard"), None)
    in_specs = (both, both, both, both, P(("blk", "shard")))
    return jax.shard_map(
        body, mesh=mesh, in_specs=in_specs, out_specs=(both, both, both), check_vma=False
    )
```

```python
import functools

import jax
import jax.numpy as jnp
from jax import lax
from jax.experimental import pallas as pl
from jax.experimental.pallas import tpu as pltpu
from jax.sharding import PartitionSpec as P

VMEM = pl.BlockSpec(memory_space=pltpu.VMEM)
ANY = pl.BlockSpec(memory_space=pl.ANY)
HBM = pl.BlockSpec(memory_space=pltpu.HBM)
PARAMS = pltpu.CompilerParams(vmem_limit_bytes=40 * 2**20)
F32, BF16 = jnp.float32, jnp.bfloat16


def cost(micros):
    return pl.CostEstimate(flops=0, bytes_accessed=int(micros * 3.69e6), transcendentals=0)


NONE = -1e30


def across(x, axis, count, distance):
    return lax.ppermute(x, axis, [(i, i ^ distance) for i in range(count)])


def shifted(x, axis, count, distance):
    return lax.ppermute(x, axis, [((i + distance) % count, i) for i in range(count)])


def after(x, *others):
    return lax.optimization_barrier((x, *others))


def dot(a, b, over):
    return lax.dot_general(a, b, (over, ((), ())), preferred_element_type=F32)


ROWS_ROWS = ((1,), (1,))
ROWS_COLS = ((1,), (0,))
COLS_COLS = ((0,), (0,))


def count_ids(chunk, ids, times_ref):
    pool_rows, rows = times_ref.shape
    ids = ids - lax.axis_index("shard") * pool_rows
    for c in range(0, pool_rows, chunk):
        slot = lax.broadcasted_iota(jnp.int32, (chunk, rows), 0) + c
        times = jnp.zeros((chunk, rows), F32)
        for k in range(ids.shape[0]):
            times = times + jnp.where(slot == ids[k : k + 1, :], 1.0, 0.0)
        times_ref[c : c + chunk, :] = times


def scores_of(chunk, scaling, q_ref, pool_ref, hard_ref, times_ref, stat_ref, ready):
    pool_rows, rows = hard_ref.shape
    top = jnp.full((1, rows), NONE, F32)
    for c in range(0, pool_rows, chunk):
        ready(c)
        score = dot(pool_ref[c : c + chunk, :], q_ref[...], ROWS_ROWS) * scaling
        score = jnp.where(times_ref[c : c + chunk, :] > 0, score, NONE)
        hard_ref[c : c + chunk, :] = score
        top = jnp.maximum(top, jnp.max(score, axis=0, keepdims=True))
    total = jnp.zeros((1, rows), F32)
    for c in range(0, pool_rows, chunk):
        part = times_ref[c : c + chunk, :] * jnp.exp(hard_ref[c : c + chunk, :] - top)
        total = total + jnp.sum(part, axis=0, keepdims=True)
    stat_ref[0:1, :] = top
    stat_ref[1:2, :] = total


def own_kernel(
    chunk, scaling, ids_ref, pos_ref, tile_ref, q_ref, pool_ref,
    tile_here, all_q_ref, pool_here, marks_ref, hard_ref, times_ref, stat_ref, sems,
):
    rows = q_ref.shape[0]
    neg_count = ids_ref.shape[0]
    half = pool_ref.shape[0] // 2
    marks = [
        pltpu.make_async_copy(ids_ref, marks_ref.at[0:neg_count, :], sems.at[0]),
        pltpu.make_async_copy(pos_ref, marks_ref.at[neg_count : neg_count + 1, :], sems.at[1]),
    ]
    others = [
        pltpu.make_async_copy(q_ref, all_q_ref.at[0:rows, :], sems.at[2]),
        pltpu.make_async_copy(tile_ref, tile_here, sems.at[3]),
    ]
    halves = [
        pltpu.make_async_copy(
            pool_ref.at[c : c + half, :], pool_here.at[c : c + half, :], sems.at[4 + c // half]
        )
        for c in (0, half)
    ]
    for copy in marks + others + halves:
        copy.start()
    for copy in marks:
        copy.wait()
    count_ids(chunk, marks_ref[0:neg_count, :], times_ref)
    for copy in others:
        copy.wait()

    def ready(c):
        if c % half == 0:
            halves[c // half].wait()

    scores_of(
        chunk, scaling, all_q_ref.at[0:rows, :], pool_here, hard_ref, times_ref, stat_ref, ready
    )


def hard_shapes(pool_rows, rows):
    return [
        pltpu.VMEM((pool_rows, rows), F32),
        pltpu.VMEM((pool_rows, rows), F32),
        pltpu.VMEM((2, rows), F32),
    ]


def own_scores(pieces, ids, pos, tile, q, pool):
    rows, features = q.shape
    pool_rows = pool.shape[0]
    chunk = min(pool_rows, 128)
    return pl.pallas_call(
        functools.partial(own_kernel, chunk, features ** (-0.5)),
        in_specs=[HBM] * 5,
        out_specs=[VMEM] * 7,
        out_shape=[
            pltpu.VMEM(tile.shape, BF16),
            pltpu.VMEM((pieces * rows, features), BF16),
            pltpu.VMEM((pool_rows, features), BF16),
            pltpu.VMEM((ids.shape[0] + 1, rows), jnp.int32),
        ]
        + hard_shapes(pool_rows, rows),
        scratch_shapes=[pltpu.SemaphoreType.DMA((6,))],
        compiler_params=PARAMS,
        cost_estimate=cost(20),
        name="own_scores",
    )(*(pltpu.with_memory_space_constraint(x, pltpu.HBM) for x in (ids, pos, tile, q, pool)))


def join_kernel(piece, q_ref, _, all_q_ref):
    rows = q_ref.shape[0]
    all_q_ref[piece * rows : (piece + 1) * rows, :] = q_ref[...]


def join_queries(piece, q, all_q):
    return pl.pallas_call(
        functools.partial(join_kernel, piece),
        in_specs=[VMEM, ANY],
        out_specs=VMEM,
        out_shape=pltpu.VMEM(all_q.shape, BF16),
        input_output_aliases={1: 0},
        compiler_params=PARAMS,
        cost_estimate=cost(20),
        name="join_queries",
    )(q, all_q)


def group_kernel(piece, chunk, scaling, marks_ref, all_q_ref, pool_ref, hard_ref, times_ref, stat_ref):
    rows = hard_ref.shape[1]
    count_ids(chunk, marks_ref[0 : marks_ref.shape[0] - 1, :], times_ref)
    scores_of(
        chunk, scaling, all_q_ref.at[piece * rows : (piece + 1) * rows, :], pool_ref,
        hard_ref, times_ref, stat_ref, lambda c: None,
    )


def group_scores(piece, marks, all_q, pool):
    pool_rows, rows = pool.shape[0], marks.shape[1]
    return pl.pallas_call(
        functools.partial(group_kernel, piece, min(pool_rows, 128), pool.shape[1] ** (-0.5)),
        in_specs=[VMEM] * 3,
        out_specs=[VMEM] * 3,
        out_shape=hard_shapes(pool_rows, rows),
        compiler_params=PARAMS,
        cost_estimate=cost(20),
        name="group_scores",
    )(marks, all_q, pool)


def score_kernel(scaling, keys_ref, q_ref, *refs):
    score_ref, part_ref = refs[-2:]
    stats = [r[...] for r in refs[:-2]]
    score = dot(keys_ref[...], q_ref[...], ROWS_ROWS) * scaling
    score_ref[...] = score
    stat = jnp.concatenate(stats, axis=1)
    hard_top, hard_sum = stat[0:1, :], stat[1:2, :]
    top = jnp.maximum(hard_top, jnp.max(score, axis=0, keepdims=True))
    part_ref[0:1, :] = top
    part_ref[1:2, :] = hard_sum * jnp.exp(hard_top - top) + jnp.sum(
        jnp.exp(score - top), axis=0, keepdims=True
    )


def passage_scores(keys, all_q, stats):
    held, group = keys.shape[0], all_q.shape[0]
    return pl.pallas_call(
        functools.partial(score_kernel, keys.shape[1] ** (-0.5)),
        in_specs=[VMEM] * (2 + len(stats)),
        out_specs=[VMEM] * 2,
        out_shape=[
            jax.ShapeDtypeStruct((held, group), F32),
            jax.ShapeDtypeStruct((2, group), F32),
        ],
        compiler_params=PARAMS,
        name="passage_scores",
    )(keys, all_q, *stats)


def weight_kernel(far, tile, owners, scaling, score_ref, q_ref, part_ref, other_ref, *refs):
    w_ref, log_ref, keep_ref, send_ref = refs[-4:]
    pos = jnp.concatenate([r[r.shape[0] - 1 :, :] for r in refs[:-4]], axis=1)
    held, group = score_ref.shape
    rows = group // owners
    if owners == 2:
        other = other_ref[...]
        parts = [
            part_ref[...],
            jnp.concatenate([other[:, rows:], other[:, :rows]], axis=1),
        ]
    else:
        parts = [other_ref[d] for d in range(owners)]
    top = functools.reduce(jnp.maximum, [p[0:1, :] for p in parts])
    total = sum(p[1:2, :] * jnp.exp(p[0:1, :] - top) for p in parts)
    log_total = top + jnp.log(total)
    log_ref[...] = log_total
    line = lax.broadcasted_iota(jnp.int32, (held, 1), 0)
    place = line // tile
    key_blk = (place % far) * 4 + ((place // far) % 2) * 2 + place // (2 * far)
    key_blk = key_blk ^ lax.axis_index("blk")
    key_id = (key_blk * owners + lax.axis_index("shard")) * tile + line % tile
    hit = jnp.where(key_id == pos, 1.0, 0.0)
    w = (jnp.exp(score_ref[...] - log_total) - hit).astype(BF16)
    w_ref[...] = w
    half = held // 2
    keep_ref[...] = dot(w[:half], q_ref[...], ROWS_COLS) * scaling
    send_ref[...] = (dot(w[half:], q_ref[...], ROWS_COLS) * scaling).astype(BF16)


def passage_weights(far, tile, owners, score, all_q, part, other, pos):
    held, group = score.shape
    features = all_q.shape[1]
    return pl.pallas_call(
        functools.partial(weight_kernel, far, tile, owners, features ** (-0.5)),
        in_specs=[VMEM] * (4 + len(pos)),
        out_specs=[VMEM] * 4,
        out_shape=[
            jax.ShapeDtypeStruct((held, group), BF16),
            jax.ShapeDtypeStruct((1, group), F32),
            jax.ShapeDtypeStruct((held // 2, features), F32),
            jax.ShapeDtypeStruct((held // 2, features), BF16),
        ],
        compiler_params=PARAMS,
        name="passage_weights",
    )(score, all_q, part, other, *pos)


def query_kernel(piece, scaling, hard_ref, times_ref, log_ref, w_ref, keys_ref, pool_ref, grad_ref, hw_ref):
    rows = hard_ref.shape[1]
    here = slice(piece * rows, (piece + 1) * rows)
    w = jnp.exp(hard_ref[...] - log_ref[:, here]).astype(BF16).astype(F32)
    hw = (times_ref[...] * w).astype(BF16)
    hw_ref[...] = hw
    grad = dot(hw, pool_ref[...], COLS_COLS) + dot(w_ref[:, here], keys_ref[...], COLS_COLS)
    grad_ref[...] = (grad * scaling).astype(grad_ref.dtype)


def query_part(piece, hard, times, log_total, w, keys, pool, dtype, micros=10):
    pool_rows, rows = hard.shape
    features = pool.shape[1]
    return pl.pallas_call(
        functools.partial(query_kernel, piece, features ** (-0.5)),
        in_specs=[VMEM] * 6,
        out_specs=[VMEM] * 2,
        out_shape=[
            jax.ShapeDtypeStruct((rows, features), dtype),
            jax.ShapeDtypeStruct((pool_rows, rows), BF16),
        ],
        compiler_params=PARAMS,
        cost_estimate=cost(micros),
        name="query_part",
    )(hard, times, log_total, w, keys, pool)


def pool_kernel(first, chunk, scaling, owners, q_ref, *refs):
    weights, (out_ref, buffer, sems) = refs[:owners], refs[-3:]
    copies = []
    for c in range(0, buffer.shape[0], chunk):
        w = jnp.concatenate([r[first + c : first + c + chunk, :] for r in weights], axis=1)
        buffer[c : c + chunk, :] = dot(w, q_ref[...], ROWS_COLS) * scaling
        copy = pltpu.make_async_copy(
            buffer.at[c : c + chunk, :],
            out_ref.at[first + c : first + c + chunk, :],
            sems.at[c // chunk],
        )
        copy.start()
        copies.append(copy)
    for copy in copies:
        copy.wait()


def pool_rows_grad(first, count, all_q, weights, so_far, micros):
    pool_rows = weights[0].shape[0]
    features = all_q.shape[1]
    chunk = min(count, 128)
    earlier = [] if so_far is None else [so_far]
    return pl.pallas_call(
        functools.partial(pool_kernel, first, chunk, features ** (-0.5), len(weights)),
        in_specs=[VMEM] * (1 + len(weights)) + [ANY] * len(earlier),
        out_specs=ANY,
        out_shape=jax.ShapeDtypeStruct((pool_rows, features), F32),
        scratch_shapes=[
            pltpu.VMEM((count, features), F32),
            pltpu.SemaphoreType.DMA((count // chunk,)),
        ],
        input_output_aliases={1 + len(weights): 0} if earlier else {},
        compiler_params=PARAMS,
        cost_estimate=cost(micros),
        name="pool_grad",
    )(all_q, *weights, *earlier)


def sum_kernel(chunk, *refs):
    terms, (out_ref, buffer, sems) = refs[:-3], refs[-3:]
    copies = []
    for c in range(0, buffer.shape[0], chunk):
        here = slice(c, c + chunk)
        buffer[here, :] = functools.reduce(jnp.add, [t[here, :].astype(F32) for t in terms])
        copy = pltpu.make_async_copy(
            buffer.at[here, :], out_ref.at[here, :], sems.at[c // chunk]
        )
        copy.start()
        copies.append(copy)
    for copy in copies:
        copy.wait()


def sum_terms(terms):
    rows = terms[0].shape[0]
    chunk = min(rows, 32)
    return pl.pallas_call(
        functools.partial(sum_kernel, chunk),
        in_specs=[VMEM] * len(terms),
        out_specs=ANY,
        out_shape=jax.ShapeDtypeStruct(terms[0].shape, F32),
        scratch_shapes=[
            pltpu.VMEM(terms[0].shape, F32),
            pltpu.SemaphoreType.DMA((rows // chunk,)),
        ],
        compiler_params=PARAMS,
        cost_estimate=cost(20),
        name="query_grad",
    )(*terms)


def body(queries, passages, neg_pool, hard_ids, positives):
    rows = queries.shape[0]
    tile = passages.shape[0]
    owners = lax.axis_size("shard")
    blocks = lax.axis_size("blk")
    my_shard = lax.axis_index("shard")

    far = blocks // 4
    far_tiles = [across(passages, "blk", blocks, 4 * z) for z in range(far - 1, 0, -1)][::-1]

    group_q = [shifted(queries, "shard", owners, d) for d in range(1, owners)]
    my_tile, all_q, pool, marks, *found = own_scores(
        owners, hard_ids.T, positives.reshape(1, rows), passages, queries, neg_pool
    )
    group_marks = [marks] + [shifted(marks, "shard", owners, d) for d in range(1, owners)]
    hard = [found]
    for d in range(1, owners):
        all_q = join_queries(d, group_q[d - 1], all_q)

    keys = jnp.concatenate([my_tile] + far_tiles, axis=0)
    keys = lax.optimization_barrier(keys)
    for bit in (2, 1):
        if bit == 1:
            keys, all_q, group_marks = after(keys, all_q, group_marks)
        keys = lax.optimization_barrier(
            jnp.concatenate([keys, across(keys, "blk", blocks, bit)], axis=0)
        )
    for d in range(1, owners):
        hard.append(group_scores(d, group_marks[d], all_q, pool))

    score, part = passage_scores(keys, all_q, [h[2] for h in hard])
    if owners == 2:
        other = shifted(part, "shard", owners, 1)
    else:
        other = lax.all_gather(jnp.roll(part, my_shard * rows, axis=1), "shard", axis=0)
        other = jnp.roll(other, -my_shard * rows, axis=2)
    w, log_total, keep, send = passage_weights(
        far, tile, owners, score, all_q, part, other, group_marks
    )

    for step, bit in enumerate((1, 2)):
        got = across(send, "blk", blocks, bit).astype(F32)
        passage_grad = keep + got
        half = passage_grad.shape[0] // 2
        keep, send = passage_grad[:half], passage_grad[half:].astype(BF16)
        if step == 0:
            made = [
                query_part(d, hard[d][0], hard[d][1], log_total, w, keys, pool, BF16)
                for d in range(1, owners)
            ]
            own, own_w = query_part(0, hard[0][0], hard[0][1], log_total, w, keys, pool, F32)
            keep, send, made, own = after(keep, send, made, own)
            back = [
                shifted(grad, "shard", owners, owners - d) for d, (grad, _) in enumerate(made, 1)
            ]
            hard_w = [own_w] + [hw for _, hw in made]
    part = neg_pool.shape[0] // 2
    pool_grad = pool_rows_grad(0, part, all_q, hard_w, None, 0.5)
    passage_grad, pool_grad = after(passage_grad, pool_grad)
    sent = passage_grad[tile:].astype(BF16)
    far_terms = [
        across(sent[(z - 1) * tile : z * tile], "blk", blocks, 4 * z)
        for z in range(far - 1, 0, -1)
    ]
    pool_grad = pool_rows_grad(part, neg_pool.shape[0] - part, all_q, hard_w, pool_grad, 20)
    query_grad = sum_terms([own] + back)
    passage_grad, pool_grad, query_grad = after(passage_grad, pool_grad, query_grad)
    passage_grad = passage_grad[:tile] + sum(t.astype(F32) for t in far_terms)

    return query_grad, passage_grad, pool_grad


def solution(mesh):
    both = P(("blk", "shard"), None)
    in_specs = (both, both, both, both, P(("blk", "shard")))
    return jax.shard_map(
        body, mesh=mesh, in_specs=in_specs, out_specs=(both, both, both), check_vma=False
    )
```

```python
import functools

import jax
import jax.numpy as jnp
from jax import lax
from jax.experimental import pallas as pl
from jax.experimental.pallas import tpu as pltpu
from jax.sharding import PartitionSpec as P

VMEM = pl.BlockSpec(memory_space=pltpu.VMEM)
ANY = pl.BlockSpec(memory_space=pl.ANY)
HBM = pl.BlockSpec(memory_space=pltpu.HBM)
PARAMS = pltpu.CompilerParams(vmem_limit_bytes=40 * 2**20)
F32, BF16 = jnp.float32, jnp.bfloat16


def cost(micros):
    return pl.CostEstimate(flops=0, bytes_accessed=int(micros * 3.69e6), transcendentals=0)


NONE = -1e30


def across(x, axis, count, distance):
    return lax.ppermute(x, axis, [(i, i ^ distance) for i in range(count)])


def shifted(x, axis, count, distance):
    return lax.ppermute(x, axis, [((i + distance) % count, i) for i in range(count)])


def after(x, *others):
    return lax.optimization_barrier((x, *others))


def dot(a, b, over):
    return lax.dot_general(a, b, (over, ((), ())), preferred_element_type=F32)


ROWS_ROWS = ((1,), (1,))
ROWS_COLS = ((1,), (0,))
COLS_COLS = ((0,), (0,))


def count_ids(chunk, ids, times_ref):
    pool_rows, rows = times_ref.shape
    ids = ids - lax.axis_index("shard") * pool_rows
    for c in range(0, pool_rows, chunk):
        slot = lax.broadcasted_iota(jnp.int32, (chunk, rows), 0) + c
        times = jnp.zeros((chunk, rows), F32)
        for k in range(ids.shape[0]):
            times = times + jnp.where(slot == ids[k : k + 1, :], 1.0, 0.0)
        times_ref[c : c + chunk, :] = times


def scores_of(chunk, scaling, q_ref, pool_ref, hard_ref, times_ref, stat_ref, ready):
    pool_rows, rows = hard_ref.shape
    top = jnp.full((1, rows), NONE, F32)
    for c in range(0, pool_rows, chunk):
        ready(c)
        score = dot(pool_ref[c : c + chunk, :], q_ref[...], ROWS_ROWS) * scaling
        score = jnp.where(times_ref[c : c + chunk, :] > 0, score, NONE)
        hard_ref[c : c + chunk, :] = score
        top = jnp.maximum(top, jnp.max(score, axis=0, keepdims=True))
    total = jnp.zeros((1, rows), F32)
    for c in range(0, pool_rows, chunk):
        part = times_ref[c : c + chunk, :] * jnp.exp(hard_ref[c : c + chunk, :] - top)
        total = total + jnp.sum(part, axis=0, keepdims=True)
    stat_ref[0:1, :] = top
    stat_ref[1:2, :] = total


def own_kernel(
    chunk, scaling, ids_ref, pos_ref, tile_ref, q_ref, pool_ref,
    tile_here, own_q_ref, pool_here, marks_ref, hard_ref, times_ref, stat_ref, sems,
):
    neg_count = ids_ref.shape[0]
    half = pool_ref.shape[0] // 2
    marks = [
        pltpu.make_async_copy(ids_ref, marks_ref.at[0:neg_count, :], sems.at[0]),
        pltpu.make_async_copy(pos_ref, marks_ref.at[neg_count : neg_count + 1, :], sems.at[1]),
    ]
    others = [
        pltpu.make_async_copy(q_ref, own_q_ref, sems.at[2]),
        pltpu.make_async_copy(tile_ref, tile_here, sems.at[3]),
    ]
    halves = [
        pltpu.make_async_copy(
            pool_ref.at[c : c + half, :], pool_here.at[c : c + half, :], sems.at[4 + c // half]
        )
        for c in (0, half)
    ]
    for copy in marks + others + halves:
        copy.start()
    for copy in marks:
        copy.wait()
    count_ids(chunk, marks_ref[0:neg_count, :], times_ref)
    for copy in others:
        copy.wait()

    def ready(c):
        if c % half == 0:
            halves[c // half].wait()

    scores_of(
        chunk, scaling, own_q_ref, pool_here, hard_ref, times_ref, stat_ref, ready
    )


def hard_shapes(pool_rows, rows):
    return [
        pltpu.VMEM((pool_rows, rows), F32),
        pltpu.VMEM((pool_rows, rows), F32),
        pltpu.VMEM((2, rows), F32),
    ]


def own_scores(ids, pos, tile, q, pool):
    rows, features = q.shape
    pool_rows = pool.shape[0]
    chunk = min(pool_rows // 2, 128)
    return pl.pallas_call(
        functools.partial(own_kernel, chunk, features ** (-0.5)),
        in_specs=[HBM] * 5,
        out_specs=[VMEM] * 7,
        out_shape=[
            pltpu.VMEM(tile.shape, BF16),
            pltpu.VMEM((rows, features), BF16),
            pltpu.VMEM((pool_rows, features), BF16),
            pltpu.VMEM((ids.shape[0] + 1, rows), jnp.int32),
        ]
        + hard_shapes(pool_rows, rows),
        scratch_shapes=[pltpu.SemaphoreType.DMA((6,))],
        compiler_params=PARAMS,
        cost_estimate=cost(20),
        name="own_scores",
    )(*(pltpu.with_memory_space_constraint(x, pltpu.HBM) for x in (ids, pos, tile, q, pool)))


def join_kernel(*refs):
    rows = refs[0].shape[0]
    for d, ref in enumerate(refs[:-1]):
        refs[-1][d * rows : (d + 1) * rows, :] = ref[...]


def join_queries(pieces):
    rows, features = pieces[0].shape
    return pl.pallas_call(
        join_kernel,
        in_specs=[VMEM] * len(pieces),
        out_specs=VMEM,
        out_shape=pltpu.VMEM((len(pieces) * rows, features), BF16),
        compiler_params=PARAMS,
        cost_estimate=cost(20),
        name="join_queries",
    )(*pieces)


def group_kernel(piece, chunk, scaling, marks_ref, all_q_ref, pool_ref, hard_ref, times_ref, stat_ref):
    rows = hard_ref.shape[1]
    count_ids(chunk, marks_ref[0 : marks_ref.shape[0] - 1, :], times_ref)
    scores_of(
        chunk, scaling, all_q_ref.at[piece * rows : (piece + 1) * rows, :], pool_ref,
        hard_ref, times_ref, stat_ref, lambda c: None,
    )


def group_scores(piece, marks, all_q, pool):
    pool_rows, rows = pool.shape[0], marks.shape[1]
    return pl.pallas_call(
        functools.partial(group_kernel, piece, min(pool_rows, 128), pool.shape[1] ** (-0.5)),
        in_specs=[VMEM] * 3,
        out_specs=[VMEM] * 3,
        out_shape=hard_shapes(pool_rows, rows),
        compiler_params=PARAMS,
        cost_estimate=cost(20),
        name="group_scores",
    )(marks, all_q, pool)


def score_kernel(scaling, keys_ref, q_ref, *refs):
    score_ref, part_ref = refs[-2:]
    stats = [r[...] for r in refs[:-2]]
    score = dot(keys_ref[...], q_ref[...], ROWS_ROWS) * scaling
    score_ref[...] = score
    stat = jnp.concatenate(stats, axis=1)
    hard_top, hard_sum = stat[0:1, :], stat[1:2, :]
    top = jnp.maximum(hard_top, jnp.max(score, axis=0, keepdims=True))
    part_ref[0:1, :] = top
    part_ref[1:2, :] = hard_sum * jnp.exp(hard_top - top) + jnp.sum(
        jnp.exp(score - top), axis=0, keepdims=True
    )


def passage_scores(keys, all_q, stats):
    held, group = keys.shape[0], all_q.shape[0]
    return pl.pallas_call(
        functools.partial(score_kernel, keys.shape[1] ** (-0.5)),
        in_specs=[VMEM] * (2 + len(stats)),
        out_specs=[VMEM] * 2,
        out_shape=[
            jax.ShapeDtypeStruct((held, group), F32),
            jax.ShapeDtypeStruct((2, group), F32),
        ],
        compiler_params=PARAMS,
        name="passage_scores",
    )(keys, all_q, *stats)


def weight_kernel(far, tile, owners, scaling, score_ref, q_ref, part_ref, other_ref, *refs):
    w_ref, log_ref, keep_ref, send_ref = refs[-4:]
    pos = jnp.concatenate([r[r.shape[0] - 1 :, :] for r in refs[:-4]], axis=1)
    held, group = score_ref.shape
    rows = group // owners
    if owners == 2:
        other = other_ref[...]
        parts = [
            part_ref[...],
            jnp.concatenate([other[:, rows:], other[:, :rows]], axis=1),
        ]
    else:
        parts = [other_ref[d] for d in range(owners)]
    top = functools.reduce(jnp.maximum, [p[0:1, :] for p in parts])
    total = sum(p[1:2, :] * jnp.exp(p[0:1, :] - top) for p in parts)
    log_total = top + jnp.log(total)
    log_ref[...] = log_total
    line = lax.broadcasted_iota(jnp.int32, (held, 1), 0)
    place = line // tile
    key_blk = (place % far) * 4 + ((place // far) % 2) * 2 + place // (2 * far)
    key_blk = key_blk ^ lax.axis_index("blk")
    key_id = (key_blk * owners + lax.axis_index("shard")) * tile + line % tile
    hit = jnp.where(key_id == pos, 1.0, 0.0)
    w = (jnp.exp(score_ref[...] - log_total) - hit).astype(BF16)
    w_ref[...] = w
    half = held // 2
    terms = dot(w, q_ref[...], ROWS_COLS) * scaling
    keep_ref[...] = terms[:half]
    send_ref[...] = terms[half:].astype(BF16)


def passage_weights(far, tile, owners, score, all_q, part, other, pos):
    held, group = score.shape
    features = all_q.shape[1]
    return pl.pallas_call(
        functools.partial(weight_kernel, far, tile, owners, features ** (-0.5)),
        in_specs=[VMEM] * (4 + len(pos)),
        out_specs=[VMEM] * 4,
        out_shape=[
            jax.ShapeDtypeStruct((held, group), BF16),
            jax.ShapeDtypeStruct((1, group), F32),
            jax.ShapeDtypeStruct((held // 2, features), F32),
            jax.ShapeDtypeStruct((held // 2, features), BF16),
        ],
        compiler_params=PARAMS,
        name="passage_weights",
    )(score, all_q, part, other, *pos)


def query_kernel(piece, scaling, hard_ref, times_ref, log_ref, w_ref, keys_ref, pool_ref, grad_ref, hw_ref):
    rows = hard_ref.shape[1]
    here = slice(piece * rows, (piece + 1) * rows)
    w = jnp.exp(hard_ref[...] - log_ref[:, here]).astype(BF16).astype(F32)
    hw = (times_ref[...] * w).astype(BF16)
    hw_ref[...] = hw
    grad = dot(hw, pool_ref[...], COLS_COLS) + dot(w_ref[:, here], keys_ref[...], COLS_COLS)
    grad_ref[...] = (grad * scaling).astype(grad_ref.dtype)


def query_part(piece, hard, times, log_total, w, keys, pool, dtype, micros=10):
    pool_rows, rows = hard.shape
    features = pool.shape[1]
    return pl.pallas_call(
        functools.partial(query_kernel, piece, features ** (-0.5)),
        in_specs=[VMEM] * 6,
        out_specs=[VMEM] * 2,
        out_shape=[
            jax.ShapeDtypeStruct((rows, features), dtype),
            jax.ShapeDtypeStruct((pool_rows, rows), BF16),
        ],
        compiler_params=PARAMS,
        cost_estimate=cost(micros),
        name="query_part",
    )(hard, times, log_total, w, keys, pool)


def pool_kernel(first, chunk, scaling, owners, q_ref, *refs):
    weights, (out_ref, buffer, sems) = refs[:owners], refs[-3:]
    copies = []
    for c in range(0, buffer.shape[0], chunk):
        w = jnp.concatenate([r[first + c : first + c + chunk, :] for r in weights], axis=1)
        buffer[c : c + chunk, :] = dot(w, q_ref[...], ROWS_COLS) * scaling
        copy = pltpu.make_async_copy(
            buffer.at[c : c + chunk, :],
            out_ref.at[first + c : first + c + chunk, :],
            sems.at[c // chunk],
        )
        copy.start()
        copies.append(copy)
    for copy in copies:
        copy.wait()


def pool_rows_grad(first, count, all_q, weights, so_far, micros):
    pool_rows = weights[0].shape[0]
    features = all_q.shape[1]
    chunk = min(count, 128)
    earlier = [] if so_far is None else [so_far]
    return pl.pallas_call(
        functools.partial(pool_kernel, first, chunk, features ** (-0.5), len(weights)),
        in_specs=[VMEM] * (1 + len(weights)) + [ANY] * len(earlier),
        out_specs=ANY,
        out_shape=jax.ShapeDtypeStruct((pool_rows, features), F32),
        scratch_shapes=[
            pltpu.VMEM((count, features), F32),
            pltpu.SemaphoreType.DMA((count // chunk,)),
        ],
        input_output_aliases={1 + len(weights): 0} if earlier else {},
        compiler_params=PARAMS,
        cost_estimate=cost(micros),
        name="pool_grad",
    )(all_q, *weights, *earlier)


def sum_kernel(chunk, *refs):
    terms, (out_ref, buffer, sems) = refs[:-3], refs[-3:]
    copies = []
    for c in range(0, buffer.shape[0], chunk):
        here = slice(c, c + chunk)
        buffer[here, :] = functools.reduce(jnp.add, [t[here, :].astype(F32) for t in terms])
        copy = pltpu.make_async_copy(
            buffer.at[here, :], out_ref.at[here, :], sems.at[c // chunk]
        )
        copy.start()
        copies.append(copy)
    for copy in copies:
        copy.wait()


def sum_terms(terms):
    rows = terms[0].shape[0]
    chunk = min(rows, 32)
    return pl.pallas_call(
        functools.partial(sum_kernel, chunk),
        in_specs=[VMEM] * len(terms),
        out_specs=ANY,
        out_shape=jax.ShapeDtypeStruct(terms[0].shape, F32),
        scratch_shapes=[
            pltpu.VMEM(terms[0].shape, F32),
            pltpu.SemaphoreType.DMA((rows // chunk,)),
        ],
        compiler_params=PARAMS,
        cost_estimate=cost(20),
        name="query_grad",
    )(*terms)


def body(queries, passages, neg_pool, hard_ids, positives):
    rows = queries.shape[0]
    tile = passages.shape[0]
    owners = lax.axis_size("shard")
    blocks = lax.axis_size("blk")
    my_shard = lax.axis_index("shard")

    far = blocks // 4
    far_tiles = [across(passages, "blk", blocks, 4 * z) for z in range(far - 1, 0, -1)][::-1]

    group_q = [shifted(queries, "shard", owners, d) for d in range(1, owners)]
    my_tile, own_q, pool, marks, *found = own_scores(
        hard_ids.T, positives.reshape(1, rows), passages, queries, neg_pool
    )
    group_marks = [marks] + [shifted(marks, "shard", owners, d) for d in range(1, owners)]
    hard = [found]
    all_q = join_queries([own_q] + group_q)

    keys = jnp.concatenate([my_tile] + far_tiles, axis=0)
    keys = lax.optimization_barrier(keys)
    for bit in (2, 1):
        if bit == 1:
            keys, all_q, group_marks = after(keys, all_q, group_marks)
        keys = lax.optimization_barrier(
            jnp.concatenate([keys, across(keys, "blk", blocks, bit)], axis=0)
        )
    for d in range(1, owners):
        hard.append(group_scores(d, group_marks[d], all_q, pool))

    score, part = passage_scores(keys, all_q, [h[2] for h in hard])
    if owners == 2:
        other = shifted(part, "shard", owners, 1)
    else:
        other = lax.all_gather(jnp.roll(part, my_shard * rows, axis=1), "shard", axis=0)
        other = jnp.roll(other, -my_shard * rows, axis=2)
    w, log_total, keep, send = passage_weights(
        far, tile, owners, score, all_q, part, other, group_marks
    )

    for step, bit in enumerate((1, 2)):
        got = across(send, "blk", blocks, bit).astype(F32)
        passage_grad = keep + got
        half = passage_grad.shape[0] // 2
        keep, send = passage_grad[:half], passage_grad[half:].astype(BF16)
        if step == 0:
            made = [
                query_part(d, hard[d][0], hard[d][1], log_total, w, keys, pool, BF16)
                for d in range(1, owners)
            ]
            own, own_w = query_part(0, hard[0][0], hard[0][1], log_total, w, keys, pool, F32)
            keep, send, made, own = after(keep, send, made, own)
            back = [
                shifted(grad, "shard", owners, owners - d) for d, (grad, _) in enumerate(made, 1)
            ]
            hard_w = [own_w] + [hw for _, hw in made]
    part = neg_pool.shape[0] // 2
    pool_grad = pool_rows_grad(0, part, all_q, hard_w, None, 20)
    passage_grad, pool_grad = after(passage_grad, pool_grad)
    sent = passage_grad[tile:].astype(BF16)
    far_terms = [
        across(sent[(z - 1) * tile : z * tile], "blk", blocks, 4 * z)
        for z in range(far - 1, 0, -1)
    ]
    pool_grad = pool_rows_grad(part, neg_pool.shape[0] - part, all_q, hard_w, pool_grad, 20)
    query_grad = sum_terms([own] + back)
    passage_grad, pool_grad, query_grad = after(passage_grad, pool_grad, query_grad)
    passage_grad = passage_grad[:tile] + sum(t.astype(F32) for t in far_terms)

    return query_grad, passage_grad, pool_grad


def solution(mesh):
    both = P(("blk", "shard"), None)
    in_specs = (both, both, both, both, P(("blk", "shard")))
    return jax.shard_map(
        body, mesh=mesh, in_specs=in_specs, out_specs=(both, both, both), check_vma=False
    )
```

```python
import functools

import jax
import jax.numpy as jnp
from jax import lax
from jax.experimental import pallas as pl
from jax.experimental.pallas import tpu as pltpu
from jax.sharding import PartitionSpec as P

VMEM = pl.BlockSpec(memory_space=pltpu.VMEM)
ANY = pl.BlockSpec(memory_space=pl.ANY)
HBM = pl.BlockSpec(memory_space=pltpu.HBM)
PARAMS = pltpu.CompilerParams(vmem_limit_bytes=40 * 2**20)
F32, BF16 = jnp.float32, jnp.bfloat16


def cost(micros):
    return pl.CostEstimate(flops=0, bytes_accessed=int(micros * 3.69e6), transcendentals=0)


NONE = -1e30


def across(x, axis, count, distance):
    return lax.ppermute(x, axis, [(i, i ^ distance) for i in range(count)])


def shifted(x, axis, count, distance):
    return lax.ppermute(x, axis, [((i + distance) % count, i) for i in range(count)])


def after(x, *others):
    return lax.optimization_barrier((x, *others))


def dot(a, b, over):
    return lax.dot_general(a, b, (over, ((), ())), preferred_element_type=F32)


ROWS_ROWS = ((1,), (1,))
ROWS_COLS = ((1,), (0,))
COLS_COLS = ((0,), (0,))


def count_ids(chunk, ids, times_ref):
    pool_rows, rows = times_ref.shape
    ids = ids - lax.axis_index("shard") * pool_rows
    for c in range(0, pool_rows, chunk):
        slot = lax.broadcasted_iota(jnp.int32, (chunk, rows), 0) + c
        times = jnp.zeros((chunk, rows), F32)
        for k in range(ids.shape[0]):
            times = times + jnp.where(slot == ids[k : k + 1, :], 1.0, 0.0)
        times_ref[c : c + chunk, :] = times


def scores_of(chunk, scaling, q_ref, pool_ref, hard_ref, times_ref, stat_ref, ready):
    pool_rows, rows = hard_ref.shape
    top = jnp.full((1, rows), NONE, F32)
    for c in range(0, pool_rows, chunk):
        ready(c)
        score = dot(pool_ref[c : c + chunk, :], q_ref[...], ROWS_ROWS) * scaling
        score = jnp.where(times_ref[c : c + chunk, :] > 0, score, NONE)
        hard_ref[c : c + chunk, :] = score
        top = jnp.maximum(top, jnp.max(score, axis=0, keepdims=True))
    total = jnp.zeros((1, rows), F32)
    for c in range(0, pool_rows, chunk):
        part = times_ref[c : c + chunk, :] * jnp.exp(hard_ref[c : c + chunk, :] - top)
        total = total + jnp.sum(part, axis=0, keepdims=True)
    stat_ref[0:1, :] = top
    stat_ref[1:2, :] = total


def own_kernel(
    chunk, scaling, ids_ref, pos_ref, tile_ref, q_ref, pool_ref,
    tile_here, own_q_ref, pool_here, marks_ref, turned_ref, hard_ref, times_ref, stat_ref, sems,
):
    neg_count = ids_ref.shape[0]
    half = pool_ref.shape[0] // 2
    marks = [
        pltpu.make_async_copy(ids_ref, marks_ref.at[0:neg_count, :], sems.at[0]),
        pltpu.make_async_copy(pos_ref, marks_ref.at[neg_count : neg_count + 1, :], sems.at[1]),
    ]
    others = [
        pltpu.make_async_copy(q_ref, own_q_ref, sems.at[2]),
        pltpu.make_async_copy(tile_ref, tile_here, sems.at[3]),
    ]
    halves = [
        pltpu.make_async_copy(
            pool_ref.at[c : c + half, :], pool_here.at[c : c + half, :], sems.at[4 + c // half]
        )
        for c in (0, half)
    ]
    for copy in marks + others + halves:
        copy.start()
    for copy in marks:
        copy.wait()
    count_ids(chunk, marks_ref[0:neg_count, :], times_ref)
    for copy in others:
        copy.wait()
    turned_ref[...] = own_q_ref[...].T

    def ready(c):
        if c % half == 0:
            halves[c // half].wait()

    scores_of(
        chunk, scaling, own_q_ref, pool_here, hard_ref, times_ref, stat_ref, ready
    )


def hard_shapes(pool_rows, rows):
    return [
        pltpu.VMEM((pool_rows, rows), F32),
        pltpu.VMEM((pool_rows, rows), F32),
        pltpu.VMEM((2, rows), F32),
    ]


def own_scores(ids, pos, tile, q, pool):
    rows, features = q.shape
    pool_rows = pool.shape[0]
    chunk = min(pool_rows // 2, 128)
    return pl.pallas_call(
        functools.partial(own_kernel, chunk, features ** (-0.5)),
        in_specs=[HBM] * 5,
        out_specs=[VMEM] * 8,
        out_shape=[
            pltpu.VMEM(tile.shape, BF16),
            pltpu.VMEM((rows, features), BF16),
            pltpu.VMEM((pool_rows, features), BF16),
            pltpu.VMEM((ids.shape[0] + 1, rows), jnp.int32),
            pltpu.VMEM((features, rows), BF16),
        ]
        + hard_shapes(pool_rows, rows),
        scratch_shapes=[pltpu.SemaphoreType.DMA((6,))],
        compiler_params=PARAMS,
        cost_estimate=cost(20),
        name="own_scores",
    )(*(pltpu.with_memory_space_constraint(x, pltpu.HBM) for x in (ids, pos, tile, q, pool)))


def join_kernel(*refs):
    rows = refs[0].shape[0]
    for d, ref in enumerate(refs[:-1]):
        refs[-1][d * rows : (d + 1) * rows, :] = ref[...]


def join_queries(pieces):
    rows, features = pieces[0].shape
    return pl.pallas_call(
        join_kernel,
        in_specs=[VMEM] * len(pieces),
        out_specs=VMEM,
        out_shape=pltpu.VMEM((len(pieces) * rows, features), BF16),
        compiler_params=PARAMS,
        cost_estimate=cost(20),
        name="join_queries",
    )(*pieces)


def group_kernel(
    piece, chunk, scaling, marks_ref, all_q_ref, pool_ref, turned_ref, hard_ref, times_ref, stat_ref
):
    rows = hard_ref.shape[1]
    turned_ref[...] = all_q_ref[piece * rows : (piece + 1) * rows, :].T
    count_ids(chunk, marks_ref[0 : marks_ref.shape[0] - 1, :], times_ref)
    scores_of(
        chunk, scaling, all_q_ref.at[piece * rows : (piece + 1) * rows, :], pool_ref,
        hard_ref, times_ref, stat_ref, lambda c: None,
    )


def group_scores(piece, marks, all_q, pool):
    pool_rows, rows = pool.shape[0], marks.shape[1]
    return pl.pallas_call(
        functools.partial(group_kernel, piece, min(pool_rows, 128), pool.shape[1] ** (-0.5)),
        in_specs=[VMEM] * 3,
        out_specs=[VMEM] * 4,
        out_shape=[pltpu.VMEM((pool.shape[1], rows), BF16)] + hard_shapes(pool_rows, rows),
        compiler_params=PARAMS,
        cost_estimate=cost(20),
        name="group_scores",
    )(marks, all_q, pool)


def score_kernel(owners, scaling, keys_ref, *refs):
    score_ref, part_ref = refs[-2:]
    turned = jnp.concatenate([r[...] for r in refs[:owners]], axis=1)
    stats = [r[...] for r in refs[owners:-2]]
    score = dot(keys_ref[...], turned, ROWS_COLS) * scaling
    score_ref[...] = score
    stat = jnp.concatenate(stats, axis=1)
    hard_top, hard_sum = stat[0:1, :], stat[1:2, :]
    top = jnp.maximum(hard_top, jnp.max(score, axis=0, keepdims=True))
    part_ref[0:1, :] = top
    part_ref[1:2, :] = hard_sum * jnp.exp(hard_top - top) + jnp.sum(
        jnp.exp(score - top), axis=0, keepdims=True
    )


def passage_scores(keys, turned, stats):
    held, group = keys.shape[0], len(turned) * turned[0].shape[1]
    return pl.pallas_call(
        functools.partial(score_kernel, len(turned), keys.shape[1] ** (-0.5)),
        in_specs=[VMEM] * (1 + len(turned) + len(stats)),
        out_specs=[VMEM] * 2,
        out_shape=[
            jax.ShapeDtypeStruct((held, group), F32),
            jax.ShapeDtypeStruct((2, group), F32),
        ],
        compiler_params=PARAMS,
        name="passage_scores",
    )(keys, *turned, *stats)


def weight_kernel(far, tile, owners, scaling, score_ref, q_ref, part_ref, other_ref, *refs):
    w_ref, log_ref, keep_ref, send_ref = refs[-4:]
    pos = jnp.concatenate([r[r.shape[0] - 1 :, :] for r in refs[:-4]], axis=1)
    held, group = score_ref.shape
    rows = group // owners
    if owners == 2:
        other = other_ref[...]
        parts = [
            part_ref[...],
            jnp.concatenate([other[:, rows:], other[:, :rows]], axis=1),
        ]
    else:
        parts = [other_ref[d] for d in range(owners)]
    top = functools.reduce(jnp.maximum, [p[0:1, :] for p in parts])
    total = sum(p[1:2, :] * jnp.exp(p[0:1, :] - top) for p in parts)
    log_total = top + jnp.log(total)
    log_ref[...] = log_total
    line = lax.broadcasted_iota(jnp.int32, (held, 1), 0)
    place = line // tile
    key_blk = (place % far) * 4 + ((place // far) % 2) * 2 + place // (2 * far)
    key_blk = key_blk ^ lax.axis_index("blk")
    key_id = (key_blk * owners + lax.axis_index("shard")) * tile + line % tile
    hit = jnp.where(key_id == pos, 1.0, 0.0)
    w = (jnp.exp(score_ref[...] - log_total) - hit).astype(BF16)
    w_ref[...] = w
    half = held // 2
    terms = dot(w, q_ref[...], ROWS_COLS) * scaling
    keep_ref[...] = terms[:half]
    send_ref[...] = terms[half:].astype(BF16)


def passage_weights(far, tile, owners, score, all_q, part, other, pos):
    held, group = score.shape
    features = all_q.shape[1]
    return pl.pallas_call(
        functools.partial(weight_kernel, far, tile, owners, features ** (-0.5)),
        in_specs=[VMEM] * (4 + len(pos)),
        out_specs=[VMEM] * 4,
        out_shape=[
            jax.ShapeDtypeStruct((held, group), BF16),
            jax.ShapeDtypeStruct((1, group), F32),
            jax.ShapeDtypeStruct((held // 2, features), F32),
            jax.ShapeDtypeStruct((held // 2, features), BF16),
        ],
        compiler_params=PARAMS,
        name="passage_weights",
    )(score, all_q, part, other, *pos)


def query_kernel(piece, scaling, hard_ref, times_ref, log_ref, w_ref, keys_ref, pool_ref, grad_ref, hw_ref):
    rows = hard_ref.shape[1]
    here = slice(piece * rows, (piece + 1) * rows)
    w = jnp.exp(hard_ref[...] - log_ref[:, here]).astype(BF16).astype(F32)
    hw = (times_ref[...] * w).astype(BF16)
    hw_ref[...] = hw
    grad = dot(hw, pool_ref[...], COLS_COLS) + dot(w_ref[:, here], keys_ref[...], COLS_COLS)
    grad_ref[...] = (grad * scaling).astype(grad_ref.dtype)


def query_part(piece, hard, times, log_total, w, keys, pool, dtype, micros=10):
    pool_rows, rows = hard.shape
    features = pool.shape[1]
    return pl.pallas_call(
        functools.partial(query_kernel, piece, features ** (-0.5)),
        in_specs=[VMEM] * 6,
        out_specs=[VMEM] * 2,
        out_shape=[
            jax.ShapeDtypeStruct((rows, features), dtype),
            jax.ShapeDtypeStruct((pool_rows, rows), BF16),
        ],
        compiler_params=PARAMS,
        cost_estimate=cost(micros),
        name="query_part",
    )(hard, times, log_total, w, keys, pool)


def pool_kernel(first, chunk, scaling, owners, q_ref, *refs):
    weights, (out_ref, buffer, sems) = refs[:owners], refs[-3:]
    copies = []
    for c in range(0, buffer.shape[0], chunk):
        w = jnp.concatenate([r[first + c : first + c + chunk, :] for r in weights], axis=1)
        buffer[c : c + chunk, :] = dot(w, q_ref[...], ROWS_COLS) * scaling
        copy = pltpu.make_async_copy(
            buffer.at[c : c + chunk, :],
            out_ref.at[first + c : first + c + chunk, :],
            sems.at[c // chunk],
        )
        copy.start()
        copies.append(copy)
    for copy in copies:
        copy.wait()


def pool_rows_grad(first, count, all_q, weights, so_far, micros):
    pool_rows = weights[0].shape[0]
    features = all_q.shape[1]
    chunk = min(count, 128)
    earlier = [] if so_far is None else [so_far]
    return pl.pallas_call(
        functools.partial(pool_kernel, first, chunk, features ** (-0.5), len(weights)),
        in_specs=[VMEM] * (1 + len(weights)) + [ANY] * len(earlier),
        out_specs=ANY,
        out_shape=jax.ShapeDtypeStruct((pool_rows, features), F32),
        scratch_shapes=[
            pltpu.VMEM((count, features), F32),
            pltpu.SemaphoreType.DMA((count // chunk,)),
        ],
        input_output_aliases={1 + len(weights): 0} if earlier else {},
        compiler_params=PARAMS,
        cost_estimate=cost(micros),
        name="pool_grad",
    )(all_q, *weights, *earlier)


def sum_kernel(chunk, *refs):
    terms, (out_ref, buffer, sems) = refs[:-3], refs[-3:]
    copies = []
    for c in range(0, buffer.shape[0], chunk):
        here = slice(c, c + chunk)
        buffer[here, :] = functools.reduce(jnp.add, [t[here, :].astype(F32) for t in terms])
        copy = pltpu.make_async_copy(
            buffer.at[here, :], out_ref.at[here, :], sems.at[c // chunk]
        )
        copy.start()
        copies.append(copy)
    for copy in copies:
        copy.wait()


def sum_terms(terms):
    rows = terms[0].shape[0]
    chunk = min(rows, 32)
    return pl.pallas_call(
        functools.partial(sum_kernel, chunk),
        in_specs=[VMEM] * len(terms),
        out_specs=ANY,
        out_shape=jax.ShapeDtypeStruct(terms[0].shape, F32),
        scratch_shapes=[
            pltpu.VMEM(terms[0].shape, F32),
            pltpu.SemaphoreType.DMA((rows // chunk,)),
        ],
        compiler_params=PARAMS,
        cost_estimate=cost(20),
        name="query_grad",
    )(*terms)


def body(queries, passages, neg_pool, hard_ids, positives):
    rows = queries.shape[0]
    tile = passages.shape[0]
    owners = lax.axis_size("shard")
    blocks = lax.axis_size("blk")
    my_shard = lax.axis_index("shard")

    far = blocks // 4
    far_tiles = [across(passages, "blk", blocks, 4 * z) for z in range(far - 1, 0, -1)][::-1]

    group_q = [shifted(queries, "shard", owners, d) for d in range(1, owners)]
    my_tile, own_q, pool, marks, own_turned, *found = own_scores(
        hard_ids.T, positives.reshape(1, rows), passages, queries, neg_pool
    )
    group_marks = [marks] + [shifted(marks, "shard", owners, d) for d in range(1, owners)]
    hard, turned = [found], [own_turned]
    all_q = join_queries([own_q] + group_q)

    keys = jnp.concatenate([my_tile] + far_tiles, axis=0)
    keys = lax.optimization_barrier(keys)
    for bit in (2, 1):
        if bit == 1:
            keys, all_q, group_marks = after(keys, all_q, group_marks)
        keys = lax.optimization_barrier(
            jnp.concatenate([keys, across(keys, "blk", blocks, bit)], axis=0)
        )
    for d in range(1, owners):
        other_turned, *found = group_scores(d, group_marks[d], all_q, pool)
        turned.append(other_turned)
        hard.append(found)

    score, part = passage_scores(keys, turned, [h[2] for h in hard])
    if owners == 2:
        other = shifted(part, "shard", owners, 1)
    else:
        other = lax.all_gather(jnp.roll(part, my_shard * rows, axis=1), "shard", axis=0)
        other = jnp.roll(other, -my_shard * rows, axis=2)
    w, log_total, keep, send = passage_weights(
        far, tile, owners, score, all_q, part, other, group_marks
    )

    for step, bit in enumerate((1, 2)):
        got = across(send, "blk", blocks, bit).astype(F32)
        passage_grad = keep + got
        half = passage_grad.shape[0] // 2
        keep, send = passage_grad[:half], passage_grad[half:].astype(BF16)
        if step == 0:
            made = [
                query_part(d, hard[d][0], hard[d][1], log_total, w, keys, pool, BF16)
                for d in range(1, owners)
            ]
            own, own_w = query_part(0, hard[0][0], hard[0][1], log_total, w, keys, pool, F32)
            keep, send, made, own = after(keep, send, made, own)
            back = [
                shifted(grad, "shard", owners, owners - d) for d, (grad, _) in enumerate(made, 1)
            ]
            hard_w = [own_w] + [hw for _, hw in made]
    part = neg_pool.shape[0] // 2
    pool_grad = pool_rows_grad(0, part, all_q, hard_w, None, 20)
    passage_grad, pool_grad = after(passage_grad, pool_grad)
    sent = passage_grad[tile:].astype(BF16)
    far_terms = [
        across(sent[(z - 1) * tile : z * tile], "blk", blocks, 4 * z)
        for z in range(far - 1, 0, -1)
    ]
    pool_grad = pool_rows_grad(part, neg_pool.shape[0] - part, all_q, hard_w, pool_grad, 20)
    query_grad = sum_terms([own] + back)
    passage_grad, pool_grad, query_grad = after(passage_grad, pool_grad, query_grad)
    passage_grad = passage_grad[:tile] + sum(t.astype(F32) for t in far_terms)

    return query_grad, passage_grad, pool_grad


def solution(mesh):
    both = P(("blk", "shard"), None)
    in_specs = (both, both, both, both, P(("blk", "shard")))
    return jax.shard_map(
        body, mesh=mesh, in_specs=in_specs, out_specs=(both, both, both), check_vma=False
    )
```

```python
import functools

import jax
import jax.numpy as jnp
from jax import lax
from jax.experimental import pallas as pl
from jax.experimental.pallas import tpu as pltpu
from jax.sharding import PartitionSpec as P

VMEM = pl.BlockSpec(memory_space=pltpu.VMEM)
ANY = pl.BlockSpec(memory_space=pl.ANY)
HBM = pl.BlockSpec(memory_space=pltpu.HBM)
PARAMS = pltpu.CompilerParams(vmem_limit_bytes=40 * 2**20)
F32, BF16 = jnp.float32, jnp.bfloat16


def cost(micros):
    return pl.CostEstimate(flops=0, bytes_accessed=int(micros * 3.69e6), transcendentals=0)


NONE = -1e30


def across(x, axis, count, distance):
    return lax.ppermute(x, axis, [(i, i ^ distance) for i in range(count)])


def shifted(x, axis, count, distance):
    return lax.ppermute(x, axis, [((i + distance) % count, i) for i in range(count)])


def after(x, *others):
    return lax.optimization_barrier((x, *others))


def dot(a, b, over):
    return lax.dot_general(a, b, (over, ((), ())), preferred_element_type=F32)


ROWS_ROWS = ((1,), (1,))
ROWS_COLS = ((1,), (0,))
COLS_COLS = ((0,), (0,))


def count_ids(chunk, ids, times_ref):
    pool_rows, rows = times_ref.shape
    ids = ids - lax.axis_index("shard") * pool_rows
    for c in range(0, pool_rows, chunk):
        slot = lax.broadcasted_iota(jnp.int32, (chunk, rows), 0) + c
        times = jnp.zeros((chunk, rows), F32)
        for k in range(ids.shape[0]):
            times = times + jnp.where(slot == ids[k : k + 1, :], 1.0, 0.0)
        times_ref[c : c + chunk, :] = times


def scores_of(chunk, scaling, q_ref, pool_ref, hard_ref, times_ref, stat_ref, ready):
    pool_rows, rows = hard_ref.shape
    top = jnp.full((1, rows), NONE, F32)
    for c in range(0, pool_rows, chunk):
        ready(c)
        score = dot(pool_ref[c : c + chunk, :], q_ref[...], ROWS_ROWS) * scaling
        score = jnp.where(times_ref[c : c + chunk, :] > 0, score, NONE)
        hard_ref[c : c + chunk, :] = score
        top = jnp.maximum(top, jnp.max(score, axis=0, keepdims=True))
    total = jnp.zeros((1, rows), F32)
    for c in range(0, pool_rows, chunk):
        part = times_ref[c : c + chunk, :] * jnp.exp(hard_ref[c : c + chunk, :] - top)
        total = total + jnp.sum(part, axis=0, keepdims=True)
    stat_ref[0:1, :] = top
    stat_ref[1:2, :] = total


def own_kernel(
    chunk, scaling, ids_ref, pos_ref, tile_ref, q_ref, pool_ref,
    tile_here, own_q_ref, pool_here, marks_ref, turned_ref, hard_ref, times_ref, stat_ref, sems,
):
    neg_count = ids_ref.shape[0]
    half = pool_ref.shape[0] // 2
    marks = [
        pltpu.make_async_copy(ids_ref, marks_ref.at[0:neg_count, :], sems.at[0]),
        pltpu.make_async_copy(pos_ref, marks_ref.at[neg_count : neg_count + 1, :], sems.at[1]),
    ]
    others = [
        pltpu.make_async_copy(q_ref, own_q_ref, sems.at[2]),
        pltpu.make_async_copy(tile_ref, tile_here, sems.at[3]),
    ]
    halves = [
        pltpu.make_async_copy(
            pool_ref.at[c : c + half, :], pool_here.at[c : c + half, :], sems.at[4 + c // half]
        )
        for c in (0, half)
    ]
    for copy in marks + others + halves:
        copy.start()
    for copy in marks:
        copy.wait()
    count_ids(chunk, marks_ref[0:neg_count, :], times_ref)
    for copy in others:
        copy.wait()
    turned_ref[...] = own_q_ref[...].T

    def ready(c):
        if c % half == 0:
            halves[c // half].wait()

    scores_of(
        chunk, scaling, own_q_ref, pool_here, hard_ref, times_ref, stat_ref, ready
    )


def hard_shapes(pool_rows, rows):
    return [
        pltpu.VMEM((pool_rows, rows), F32),
        pltpu.VMEM((pool_rows, rows), F32),
        pltpu.VMEM((2, rows), F32),
    ]


def own_scores(ids, pos, tile, q, pool):
    rows, features = q.shape
    pool_rows = pool.shape[0]
    chunk = min(pool_rows // 2, 128)
    return pl.pallas_call(
        functools.partial(own_kernel, chunk, features ** (-0.5)),
        in_specs=[HBM] * 5,
        out_specs=[VMEM] * 8,
        out_shape=[
            pltpu.VMEM(tile.shape, BF16),
            pltpu.VMEM((rows, features), BF16),
            pltpu.VMEM((pool_rows, features), BF16),
            pltpu.VMEM((ids.shape[0] + 1, rows), jnp.int32),
            pltpu.VMEM((features, rows), BF16),
        ]
        + hard_shapes(pool_rows, rows),
        scratch_shapes=[pltpu.SemaphoreType.DMA((6,))],
        compiler_params=PARAMS,
        cost_estimate=cost(20),
        name="own_scores",
    )(*(pltpu.with_memory_space_constraint(x, pltpu.HBM) for x in (ids, pos, tile, q, pool)))


def join_kernel(*refs):
    rows = refs[0].shape[0]
    for d, ref in enumerate(refs[:-1]):
        refs[-1][d * rows : (d + 1) * rows, :] = ref[...]


def join_queries(pieces):
    rows, features = pieces[0].shape
    return pl.pallas_call(
        join_kernel,
        in_specs=[VMEM] * len(pieces),
        out_specs=VMEM,
        out_shape=pltpu.VMEM((len(pieces) * rows, features), BF16),
        compiler_params=PARAMS,
        cost_estimate=cost(20),
        name="join_queries",
    )(*pieces)


def group_kernel(
    piece, chunk, scaling, marks_ref, all_q_ref, pool_ref, turned_ref, hard_ref, times_ref, stat_ref
):
    rows = hard_ref.shape[1]
    turned_ref[...] = all_q_ref[piece * rows : (piece + 1) * rows, :].T
    count_ids(chunk, marks_ref[0 : marks_ref.shape[0] - 1, :], times_ref)
    scores_of(
        chunk, scaling, all_q_ref.at[piece * rows : (piece + 1) * rows, :], pool_ref,
        hard_ref, times_ref, stat_ref, lambda c: None,
    )


def group_scores(piece, marks, all_q, pool):
    pool_rows, rows = pool.shape[0], marks.shape[1]
    return pl.pallas_call(
        functools.partial(group_kernel, piece, min(pool_rows, 128), pool.shape[1] ** (-0.5)),
        in_specs=[VMEM] * 3,
        out_specs=[VMEM] * 4,
        out_shape=[pltpu.VMEM((pool.shape[1], rows), BF16)] + hard_shapes(pool_rows, rows),
        compiler_params=PARAMS,
        cost_estimate=cost(20),
        name="group_scores",
    )(marks, all_q, pool)


def score_kernel(owners, scaling, keys_ref, *refs):
    score_ref, part_ref = refs[-2:]
    turned = jnp.concatenate([r[...] for r in refs[:owners]], axis=1)
    stats = [r[...] for r in refs[owners:-2]]
    score = dot(keys_ref[...], turned, ROWS_COLS) * scaling
    score_ref[...] = score
    stat = jnp.concatenate(stats, axis=1)
    hard_top, hard_sum = stat[0:1, :], stat[1:2, :]
    top = jnp.maximum(hard_top, jnp.max(score, axis=0, keepdims=True))
    part_ref[0:1, :] = top
    part_ref[1:2, :] = hard_sum * jnp.exp(hard_top - top) + jnp.sum(
        jnp.exp(score - top), axis=0, keepdims=True
    )


def passage_scores(keys, turned, stats):
    held, group = keys.shape[0], len(turned) * turned[0].shape[1]
    return pl.pallas_call(
        functools.partial(score_kernel, len(turned), keys.shape[1] ** (-0.5)),
        in_specs=[VMEM] * (1 + len(turned) + len(stats)),
        out_specs=[VMEM] * 2,
        out_shape=[
            jax.ShapeDtypeStruct((held, group), F32),
            jax.ShapeDtypeStruct((2, group), F32),
        ],
        compiler_params=PARAMS,
        name="passage_scores",
    )(keys, *turned, *stats)


def weight_kernel(far, tile, owners, scaling, score_ref, q_ref, part_ref, other_ref, *refs):
    w_ref, log_ref, keep_ref, send_ref = refs[-4:]
    pos = jnp.concatenate([r[r.shape[0] - 1 :, :] for r in refs[:-4]], axis=1)
    held, group = score_ref.shape
    rows = group // owners
    if owners == 2:
        other = other_ref[...]
        parts = [
            part_ref[...],
            jnp.concatenate([other[:, rows:], other[:, :rows]], axis=1),
        ]
    else:
        parts = [other_ref[d] for d in range(owners)]
    top = functools.reduce(jnp.maximum, [p[0:1, :] for p in parts])
    total = sum(p[1:2, :] * jnp.exp(p[0:1, :] - top) for p in parts)
    log_total = top + jnp.log(total)
    log_ref[...] = log_total
    line = lax.broadcasted_iota(jnp.int32, (held, 1), 0)
    place = line // tile
    key_blk = (place % far) * 4 + ((place // far) % 2) * 2 + place // (2 * far)
    key_blk = key_blk ^ lax.axis_index("blk")
    key_id = (key_blk * owners + lax.axis_index("shard")) * tile + line % tile
    hit = jnp.where(key_id == pos, 1.0, 0.0)
    w = (jnp.exp(score_ref[...] - log_total) - hit).astype(BF16)
    w_ref[...] = w
    half = held // 2
    terms = dot(w, q_ref[...], ROWS_COLS) * scaling
    keep_ref[...] = terms[:half]
    send_ref[...] = terms[half:].astype(BF16)


def passage_weights(far, tile, owners, score, all_q, part, other, pos):
    held, group = score.shape
    features = all_q.shape[1]
    return pl.pallas_call(
        functools.partial(weight_kernel, far, tile, owners, features ** (-0.5)),
        in_specs=[VMEM] * (4 + len(pos)),
        out_specs=[VMEM] * 4,
        out_shape=[
            jax.ShapeDtypeStruct((held, group), BF16),
            jax.ShapeDtypeStruct((1, group), F32),
            jax.ShapeDtypeStruct((held // 2, features), F32),
            jax.ShapeDtypeStruct((held // 2, features), BF16),
        ],
        compiler_params=PARAMS,
        name="passage_weights",
    )(score, all_q, part, other, *pos)


def query_kernel(piece, scaling, hard_ref, times_ref, log_ref, w_ref, keys_ref, pool_ref, grad_ref, hw_ref):
    rows = hard_ref.shape[1]
    here = slice(piece * rows, (piece + 1) * rows)
    w = jnp.exp(hard_ref[...] - log_ref[:, here]).astype(BF16).astype(F32)
    hw = (times_ref[...] * w).astype(BF16)
    hw_ref[...] = hw
    grad = dot(hw, pool_ref[...], COLS_COLS) + dot(w_ref[:, here], keys_ref[...], COLS_COLS)
    grad_ref[...] = (grad * scaling).astype(grad_ref.dtype)


def query_part(piece, hard, times, log_total, w, keys, pool, dtype, micros=10):
    pool_rows, rows = hard.shape
    features = pool.shape[1]
    return pl.pallas_call(
        functools.partial(query_kernel, piece, features ** (-0.5)),
        in_specs=[VMEM] * 6,
        out_specs=[VMEM] * 2,
        out_shape=[
            jax.ShapeDtypeStruct((rows, features), dtype),
            jax.ShapeDtypeStruct((pool_rows, rows), BF16),
        ],
        compiler_params=PARAMS,
        cost_estimate=cost(micros),
        name="query_part",
    )(hard, times, log_total, w, keys, pool)


def pool_kernel(first, chunk, scaling, owners, q_ref, *refs):
    weights, (out_ref, buffer, sems) = refs[:owners], refs[-3:]
    copies = []
    for c in range(0, buffer.shape[0], chunk):
        w = jnp.concatenate([r[first + c : first + c + chunk, :] for r in weights], axis=1)
        buffer[c : c + chunk, :] = dot(w, q_ref[...], ROWS_COLS) * scaling
        copy = pltpu.make_async_copy(
            buffer.at[c : c + chunk, :],
            out_ref.at[first + c : first + c + chunk, :],
            sems.at[c // chunk],
        )
        copy.start()
        copies.append(copy)
    for copy in copies:
        copy.wait()


def pool_rows_grad(first, count, all_q, weights, so_far, micros):
    pool_rows = weights[0].shape[0]
    features = all_q.shape[1]
    chunk = min(count, 128)
    earlier = [] if so_far is None else [so_far]
    return pl.pallas_call(
        functools.partial(pool_kernel, first, chunk, features ** (-0.5), len(weights)),
        in_specs=[VMEM] * (1 + len(weights)) + [ANY] * len(earlier),
        out_specs=ANY,
        out_shape=jax.ShapeDtypeStruct((pool_rows, features), F32),
        scratch_shapes=[
            pltpu.VMEM((count, features), F32),
            pltpu.SemaphoreType.DMA((count // chunk,)),
        ],
        input_output_aliases={1 + len(weights): 0} if earlier else {},
        compiler_params=PARAMS,
        cost_estimate=cost(micros),
        name="pool_grad",
    )(all_q, *weights, *earlier)


def sum_kernel(chunk, *refs):
    terms, (out_ref, buffer, sems) = refs[:-3], refs[-3:]
    copies = []
    for c in range(0, buffer.shape[0], chunk):
        here = slice(c, c + chunk)
        buffer[here, :] = functools.reduce(jnp.add, [t[here, :].astype(F32) for t in terms])
        copy = pltpu.make_async_copy(
            buffer.at[here, :], out_ref.at[here, :], sems.at[c // chunk]
        )
        copy.start()
        copies.append(copy)
    for copy in copies:
        copy.wait()


def sum_terms(terms):
    rows = terms[0].shape[0]
    chunk = min(rows, 16)
    return pl.pallas_call(
        functools.partial(sum_kernel, chunk),
        in_specs=[VMEM] * len(terms),
        out_specs=ANY,
        out_shape=jax.ShapeDtypeStruct(terms[0].shape, F32),
        scratch_shapes=[
            pltpu.VMEM(terms[0].shape, F32),
            pltpu.SemaphoreType.DMA((rows // chunk,)),
        ],
        compiler_params=PARAMS,
        cost_estimate=cost(20),
        name="query_grad",
    )(*terms)


def body(queries, passages, neg_pool, hard_ids, positives):
    rows = queries.shape[0]
    tile = passages.shape[0]
    owners = lax.axis_size("shard")
    blocks = lax.axis_size("blk")
    my_shard = lax.axis_index("shard")

    far = blocks // 4
    far_tiles = [across(passages, "blk", blocks, 4 * z) for z in range(far - 1, 0, -1)][::-1]

    group_q = [shifted(queries, "shard", owners, d) for d in range(1, owners)]
    my_tile, own_q, pool, marks, own_turned, *found = own_scores(
        hard_ids.T, positives.reshape(1, rows), passages, queries, neg_pool
    )
    group_marks = [marks] + [shifted(marks, "shard", owners, d) for d in range(1, owners)]
    hard, turned = [found], [own_turned]
    all_q = join_queries([own_q] + group_q)

    keys = jnp.concatenate([my_tile] + far_tiles, axis=0)
    keys = lax.optimization_barrier(keys)
    for bit in (2, 1):
        if bit == 1:
            keys, all_q, group_marks = after(keys, all_q, group_marks)
        keys = lax.optimization_barrier(
            jnp.concatenate([keys, across(keys, "blk", blocks, bit)], axis=0)
        )
    for d in range(1, owners):
        other_turned, *found = group_scores(d, group_marks[d], all_q, pool)
        turned.append(other_turned)
        hard.append(found)

    score, part = passage_scores(keys, turned, [h[2] for h in hard])
    if owners == 2:
        other = shifted(part, "shard", owners, 1)
    else:
        other = lax.all_gather(jnp.roll(part, my_shard * rows, axis=1), "shard", axis=0)
        other = jnp.roll(other, -my_shard * rows, axis=2)
    w, log_total, keep, send = passage_weights(
        far, tile, owners, score, all_q, part, other, group_marks
    )

    for step, bit in enumerate((1, 2)):
        got = across(send, "blk", blocks, bit).astype(F32)
        passage_grad = keep + got
        half = passage_grad.shape[0] // 2
        keep, send = passage_grad[:half], passage_grad[half:].astype(BF16)
        if step == 0:
            made = [
                query_part(d, hard[d][0], hard[d][1], log_total, w, keys, pool, BF16)
                for d in range(1, owners)
            ]
            own, own_w = query_part(0, hard[0][0], hard[0][1], log_total, w, keys, pool, F32)
            keep, send, made, own = after(keep, send, made, own)
            back = [
                shifted(grad, "shard", owners, owners - d) for d, (grad, _) in enumerate(made, 1)
            ]
            hard_w = [own_w] + [hw for _, hw in made]
    part = neg_pool.shape[0] // 2
    pool_grad = pool_rows_grad(0, part, all_q, hard_w, None, 20)
    passage_grad, pool_grad = after(passage_grad, pool_grad)
    sent = passage_grad[tile:].astype(BF16)
    far_terms = [
        across(sent[(z - 1) * tile : z * tile], "blk", blocks, 4 * z)
        for z in range(far - 1, 0, -1)
    ]
    pool_grad = pool_rows_grad(part, neg_pool.shape[0] - part, all_q, hard_w, pool_grad, 20)
    query_grad = sum_terms([own] + back)
    passage_grad, pool_grad, query_grad = after(passage_grad, pool_grad, query_grad)
    passage_grad = passage_grad[:tile] + sum(t.astype(F32) for t in far_terms)

    return query_grad, passage_grad, pool_grad


def solution(mesh):
    both = P(("blk", "shard"), None)
    in_specs = (both, both, both, both, P(("blk", "shard")))
    return jax.shard_map(
        body, mesh=mesh, in_specs=in_specs, out_specs=(both, both, both), check_vma=False
    )
```

```python
import functools

import jax
import jax.numpy as jnp
from jax import lax
from jax.experimental import pallas as pl
from jax.experimental.pallas import tpu as pltpu
from jax.sharding import PartitionSpec as P

VMEM = pl.BlockSpec(memory_space=pltpu.VMEM)
ANY = pl.BlockSpec(memory_space=pl.ANY)
HBM = pl.BlockSpec(memory_space=pltpu.HBM)
PARAMS = pltpu.CompilerParams(vmem_limit_bytes=40 * 2**20)
F32, BF16 = jnp.float32, jnp.bfloat16


def cost(micros):
    return pl.CostEstimate(flops=0, bytes_accessed=int(micros * 3.69e6), transcendentals=0)


NONE = -1e30


def across(x, axis, count, distance):
    return lax.ppermute(x, axis, [(i, i ^ distance) for i in range(count)])


def shifted(x, axis, count, distance):
    return lax.ppermute(x, axis, [((i + distance) % count, i) for i in range(count)])


def after(x, *others):
    return lax.optimization_barrier((x, *others))


def dot(a, b, over):
    return lax.dot_general(a, b, (over, ((), ())), preferred_element_type=F32)


ROWS_ROWS = ((1,), (1,))
ROWS_COLS = ((1,), (0,))
COLS_COLS = ((0,), (0,))


def count_ids(chunk, ids, times_ref):
    pool_rows, rows = times_ref.shape
    ids = ids - lax.axis_index("shard") * pool_rows
    for c in range(0, pool_rows, chunk):
        slot = lax.broadcasted_iota(jnp.int32, (chunk, rows), 0) + c
        times = jnp.zeros((chunk, rows), F32)
        for k in range(ids.shape[0]):
            times = times + jnp.where(slot == ids[k : k + 1, :], 1.0, 0.0)
        times_ref[c : c + chunk, :] = times


def scores_of(chunk, scaling, q_ref, pool_ref, hard_ref, times_ref, stat_ref, ready):
    pool_rows, rows = hard_ref.shape
    top = jnp.full((1, rows), NONE, F32)
    for c in range(0, pool_rows, chunk):
        ready(c)
        score = dot(pool_ref[c : c + chunk, :], q_ref[...], ROWS_ROWS) * scaling
        score = jnp.where(times_ref[c : c + chunk, :] > 0, score, NONE)
        hard_ref[c : c + chunk, :] = score
        top = jnp.maximum(top, jnp.max(score, axis=0, keepdims=True))
    total = jnp.zeros((1, rows), F32)
    for c in range(0, pool_rows, chunk):
        part = times_ref[c : c + chunk, :] * jnp.exp(hard_ref[c : c + chunk, :] - top)
        total = total + jnp.sum(part, axis=0, keepdims=True)
    stat_ref[0:1, :] = top
    stat_ref[1:2, :] = total


def own_kernel(
    chunk, scaling, ids_ref, pos_ref, tile_ref, q_ref, pool_ref,
    tile_here, own_q_ref, pool_here, marks_ref, turned_ref, hard_ref, times_ref, stat_ref, sems,
):
    neg_count = ids_ref.shape[0]
    half = pool_ref.shape[0] // 2
    marks = [
        pltpu.make_async_copy(ids_ref, marks_ref.at[0:neg_count, :], sems.at[0]),
        pltpu.make_async_copy(pos_ref, marks_ref.at[neg_count : neg_count + 1, :], sems.at[1]),
    ]
    others = [
        pltpu.make_async_copy(q_ref, own_q_ref, sems.at[2]),
        pltpu.make_async_copy(tile_ref, tile_here, sems.at[3]),
    ]
    halves = [
        pltpu.make_async_copy(
            pool_ref.at[c : c + half, :], pool_here.at[c : c + half, :], sems.at[4 + c // half]
        )
        for c in (0, half)
    ]
    for copy in marks + others + halves:
        copy.start()
    for copy in marks:
        copy.wait()
    count_ids(chunk, marks_ref[0:neg_count, :], times_ref)
    for copy in others:
        copy.wait()
    turned_ref[...] = own_q_ref[...].T

    def ready(c):
        if c % half == 0:
            halves[c // half].wait()

    scores_of(
        chunk, scaling, own_q_ref, pool_here, hard_ref, times_ref, stat_ref, ready
    )


def hard_shapes(pool_rows, rows):
    return [
        pltpu.VMEM((pool_rows, rows), F32),
        pltpu.VMEM((pool_rows, rows), F32),
        pltpu.VMEM((2, rows), F32),
    ]


def own_scores(ids, pos, tile, q, pool):
    rows, features = q.shape
    pool_rows = pool.shape[0]
    chunk = min(pool_rows // 2, 128)
    return pl.pallas_call(
        functools.partial(own_kernel, chunk, features ** (-0.5)),
        in_specs=[HBM] * 5,
        out_specs=[VMEM] * 8,
        out_shape=[
            pltpu.VMEM(tile.shape, BF16),
            pltpu.VMEM((rows, features), BF16),
            pltpu.VMEM((pool_rows, features), BF16),
            pltpu.VMEM((ids.shape[0] + 1, rows), jnp.int32),
            pltpu.VMEM((features, rows), BF16),
        ]
        + hard_shapes(pool_rows, rows),
        scratch_shapes=[pltpu.SemaphoreType.DMA((6,))],
        compiler_params=PARAMS,
        cost_estimate=cost(20),
        name="own_scores",
    )(*(pltpu.with_memory_space_constraint(x, pltpu.HBM) for x in (ids, pos, tile, q, pool)))


def join_kernel(*refs):
    rows = refs[0].shape[0]
    for d, ref in enumerate(refs[:-1]):
        refs[-1][d * rows : (d + 1) * rows, :] = ref[...]


def join_queries(pieces):
    rows, features = pieces[0].shape
    return pl.pallas_call(
        join_kernel,
        in_specs=[VMEM] * len(pieces),
        out_specs=VMEM,
        out_shape=pltpu.VMEM((len(pieces) * rows, features), BF16),
        compiler_params=PARAMS,
        cost_estimate=cost(20),
        name="join_queries",
    )(*pieces)


def group_kernel(
    piece, chunk, scaling, marks_ref, all_q_ref, pool_ref, turned_ref, hard_ref, times_ref, stat_ref
):
    rows = hard_ref.shape[1]
    turned_ref[...] = all_q_ref[piece * rows : (piece + 1) * rows, :].T
    count_ids(chunk, marks_ref[0 : marks_ref.shape[0] - 1, :], times_ref)
    scores_of(
        chunk, scaling, all_q_ref.at[piece * rows : (piece + 1) * rows, :], pool_ref,
        hard_ref, times_ref, stat_ref, lambda c: None,
    )


def group_scores(piece, marks, all_q, pool):
    pool_rows, rows = pool.shape[0], marks.shape[1]
    return pl.pallas_call(
        functools.partial(group_kernel, piece, min(pool_rows, 128), pool.shape[1] ** (-0.5)),
        in_specs=[VMEM] * 3,
        out_specs=[VMEM] * 4,
        out_shape=[pltpu.VMEM((pool.shape[1], rows), BF16)] + hard_shapes(pool_rows, rows),
        compiler_params=PARAMS,
        cost_estimate=cost(20),
        name="group_scores",
    )(marks, all_q, pool)


def score_kernel(owners, scaling, keys_ref, *refs):
    score_ref, part_ref = refs[-2:]
    turned = jnp.concatenate([r[...] for r in refs[:owners]], axis=1)
    stats = [r[...] for r in refs[owners:-2]]
    score = dot(keys_ref[...], turned, ROWS_COLS) * scaling
    score_ref[...] = score
    stat = jnp.concatenate(stats, axis=1)
    hard_top, hard_sum = stat[0:1, :], stat[1:2, :]
    top = jnp.maximum(hard_top, jnp.max(score, axis=0, keepdims=True))
    part_ref[0:1, :] = top
    part_ref[1:2, :] = hard_sum * jnp.exp(hard_top - top) + jnp.sum(
        jnp.exp(score - top), axis=0, keepdims=True
    )


def passage_scores(keys, turned, stats):
    held, group = keys.shape[0], len(turned) * turned[0].shape[1]
    return pl.pallas_call(
        functools.partial(score_kernel, len(turned), keys.shape[1] ** (-0.5)),
        in_specs=[VMEM] * (1 + len(turned) + len(stats)),
        out_specs=[VMEM] * 2,
        out_shape=[
            jax.ShapeDtypeStruct((held, group), F32),
            jax.ShapeDtypeStruct((2, group), F32),
        ],
        compiler_params=PARAMS,
        name="passage_scores",
    )(keys, *turned, *stats)


def weight_kernel(far, tile, owners, scaling, score_ref, q_ref, part_ref, other_ref, *refs):
    w_ref, log_ref, keep_ref, send_ref = refs[-4:]
    pos = jnp.concatenate([r[r.shape[0] - 1 :, :] for r in refs[:-4]], axis=1)
    held, group = score_ref.shape
    rows = group // owners
    if owners == 2:
        other = other_ref[...]
        parts = [
            part_ref[...],
            jnp.concatenate([other[:, rows:], other[:, :rows]], axis=1),
        ]
    else:
        parts = [other_ref[d] for d in range(owners)]
    top = functools.reduce(jnp.maximum, [p[0:1, :] for p in parts])
    total = sum(p[1:2, :] * jnp.exp(p[0:1, :] - top) for p in parts)
    log_total = top + jnp.log(total)
    log_ref[...] = log_total
    line = lax.broadcasted_iota(jnp.int32, (held, 1), 0)
    place = line // tile
    key_blk = (place % far) * 4 + ((place // far) % 2) * 2 + place // (2 * far)
    key_blk = key_blk ^ lax.axis_index("blk")
    key_id = (key_blk * owners + lax.axis_index("shard")) * tile + line % tile
    hit = jnp.where(key_id == pos, 1.0, 0.0)
    w = (jnp.exp(score_ref[...] - log_total) - hit).astype(BF16)
    w_ref[...] = w
    half = held // 2
    terms = dot(w, q_ref[...], ROWS_COLS) * scaling
    keep_ref[...] = terms[:half]
    send_ref[...] = terms[half:].astype(BF16)


def passage_weights(far, tile, owners, score, all_q, part, other, pos):
    held, group = score.shape
    features = all_q.shape[1]
    return pl.pallas_call(
        functools.partial(weight_kernel, far, tile, owners, features ** (-0.5)),
        in_specs=[VMEM] * (4 + len(pos)),
        out_specs=[VMEM] * 4,
        out_shape=[
            jax.ShapeDtypeStruct((held, group), BF16),
            jax.ShapeDtypeStruct((1, group), F32),
            jax.ShapeDtypeStruct((held // 2, features), F32),
            jax.ShapeDtypeStruct((held // 2, features), BF16),
        ],
        compiler_params=PARAMS,
        name="passage_weights",
    )(score, all_q, part, other, *pos)


def query_kernel(piece, scaling, hard_ref, times_ref, log_ref, w_ref, keys_ref, pool_ref, grad_ref, hw_ref):
    rows = hard_ref.shape[1]
    here = slice(piece * rows, (piece + 1) * rows)
    w = jnp.exp(hard_ref[...] - log_ref[:, here]).astype(BF16).astype(F32)
    hw = (times_ref[...] * w).astype(BF16)
    hw_ref[...] = hw
    grad = dot(hw, pool_ref[...], COLS_COLS) + dot(w_ref[:, here], keys_ref[...], COLS_COLS)
    grad_ref[...] = (grad * scaling).astype(grad_ref.dtype)


def query_part(piece, hard, times, log_total, w, keys, pool, dtype, micros=10):
    pool_rows, rows = hard.shape
    features = pool.shape[1]
    return pl.pallas_call(
        functools.partial(query_kernel, piece, features ** (-0.5)),
        in_specs=[VMEM] * 6,
        out_specs=[VMEM] * 2,
        out_shape=[
            jax.ShapeDtypeStruct((rows, features), dtype),
            jax.ShapeDtypeStruct((pool_rows, rows), BF16),
        ],
        compiler_params=PARAMS,
        cost_estimate=cost(micros),
        name="query_part",
    )(hard, times, log_total, w, keys, pool)


def pool_kernel(first, chunk, scaling, owners, q_ref, *refs):
    weights, (out_ref, buffer, sems) = refs[:owners], refs[-3:]
    copies = []
    for c in range(0, buffer.shape[0], chunk):
        w = jnp.concatenate([r[first + c : first + c + chunk, :] for r in weights], axis=1)
        buffer[c : c + chunk, :] = dot(w, q_ref[...], ROWS_COLS) * scaling
        copy = pltpu.make_async_copy(
            buffer.at[c : c + chunk, :],
            out_ref.at[first + c : first + c + chunk, :],
            sems.at[c // chunk],
        )
        copy.start()
        copies.append(copy)
    for copy in copies:
        copy.wait()


def pool_rows_grad(first, count, all_q, weights, so_far, micros):
    pool_rows = weights[0].shape[0]
    features = all_q.shape[1]
    chunk = min(count, 128)
    earlier = [] if so_far is None else [so_far]
    return pl.pallas_call(
        functools.partial(pool_kernel, first, chunk, features ** (-0.5), len(weights)),
        in_specs=[VMEM] * (1 + len(weights)) + [ANY] * len(earlier),
        out_specs=ANY,
        out_shape=jax.ShapeDtypeStruct((pool_rows, features), F32),
        scratch_shapes=[
            pltpu.VMEM((count, features), F32),
            pltpu.SemaphoreType.DMA((count // chunk,)),
        ],
        input_output_aliases={1 + len(weights): 0} if earlier else {},
        compiler_params=PARAMS,
        cost_estimate=cost(micros),
        name="pool_grad",
    )(all_q, *weights, *earlier)


def sum_kernel(chunk, *refs):
    terms, (out_ref, buffer, sems) = refs[:-3], refs[-3:]
    copies = []
    for c in range(0, buffer.shape[0], chunk):
        here = slice(c, c + chunk)
        buffer[here, :] = functools.reduce(jnp.add, [t[here, :].astype(F32) for t in terms])
        copy = pltpu.make_async_copy(
            buffer.at[here, :], out_ref.at[here, :], sems.at[c // chunk]
        )
        copy.start()
        copies.append(copy)
    for copy in copies:
        copy.wait()


def sum_terms(terms):
    rows = terms[0].shape[0]
    chunk = min(rows, 16)
    return pl.pallas_call(
        functools.partial(sum_kernel, chunk),
        in_specs=[VMEM] * len(terms),
        out_specs=ANY,
        out_shape=jax.ShapeDtypeStruct(terms[0].shape, F32),
        scratch_shapes=[
            pltpu.VMEM(terms[0].shape, F32),
            pltpu.SemaphoreType.DMA((rows // chunk,)),
        ],
        compiler_params=PARAMS,
        cost_estimate=cost(20),
        name="query_grad",
    )(*terms)


def body(queries, passages, neg_pool, hard_ids, positives):
    rows = queries.shape[0]
    tile = passages.shape[0]
    owners = lax.axis_size("shard")
    blocks = lax.axis_size("blk")
    my_shard = lax.axis_index("shard")

    far = blocks // 4
    far_tiles = [across(passages, "blk", blocks, 4 * z) for z in range(far - 1, 0, -1)][::-1]

    group_q = [shifted(queries, "shard", owners, d) for d in range(1, owners)]
    my_tile, own_q, pool, marks, own_turned, *found = own_scores(
        hard_ids.T, positives.reshape(1, rows), passages, queries, neg_pool
    )
    group_marks = [marks] + [shifted(marks, "shard", owners, d) for d in range(1, owners)]
    hard, turned = [found], [own_turned]
    all_q = join_queries([own_q] + group_q)

    keys = jnp.concatenate([my_tile] + far_tiles, axis=0)
    keys = lax.optimization_barrier(keys)
    for bit in (2, 1):
        if bit == 1:
            keys, all_q, group_marks = after(keys, all_q, group_marks)
        keys = lax.optimization_barrier(
            jnp.concatenate([keys, across(keys, "blk", blocks, bit)], axis=0)
        )
    for d in range(1, owners):
        other_turned, *found = group_scores(d, group_marks[d], all_q, pool)
        turned.append(other_turned)
        hard.append(found)

    score, part = passage_scores(keys, turned, [h[2] for h in hard])
    if owners == 2:
        other = shifted(part, "shard", owners, 1)
    else:
        other = lax.all_gather(jnp.roll(part, my_shard * rows, axis=1), "shard", axis=0)
        other = jnp.roll(other, -my_shard * rows, axis=2)
    w, log_total, keep, send = passage_weights(
        far, tile, owners, score, all_q, part, other, group_marks
    )

    for step, bit in enumerate((1, 2)):
        got = across(send, "blk", blocks, bit).astype(F32)
        passage_grad = keep + got
        half = passage_grad.shape[0] // 2
        keep, send = passage_grad[:half], passage_grad[half:].astype(BF16)
        if step == 0:
            made = [
                query_part(d, hard[d][0], hard[d][1], log_total, w, keys, pool, BF16)
                for d in range(1, owners)
            ]
            own, own_w = query_part(0, hard[0][0], hard[0][1], log_total, w, keys, pool, F32)
            keep, send, made, own = after(keep, send, made, own)
            back = [
                shifted(grad, "shard", owners, owners - d) for d, (grad, _) in enumerate(made, 1)
            ]
            hard_w = [own_w] + [hw for _, hw in made]
    part = 3 * neg_pool.shape[0] // 8
    pool_grad = pool_rows_grad(0, part, all_q, hard_w, None, 20)
    passage_grad, pool_grad = after(passage_grad, pool_grad)
    sent = passage_grad[tile:].astype(BF16)
    far_terms = [
        across(sent[(z - 1) * tile : z * tile], "blk", blocks, 4 * z)
        for z in range(far - 1, 0, -1)
    ]
    pool_grad = pool_rows_grad(part, neg_pool.shape[0] - part, all_q, hard_w, pool_grad, 20)
    query_grad = sum_terms([own] + back)
    passage_grad, pool_grad, query_grad = after(passage_grad, pool_grad, query_grad)
    passage_grad = passage_grad[:tile] + sum(t.astype(F32) for t in far_terms)

    return query_grad, passage_grad, pool_grad


def solution(mesh):
    both = P(("blk", "shard"), None)
    in_specs = (both, both, both, both, P(("blk", "shard")))
    return jax.shard_map(
        body, mesh=mesh, in_specs=in_specs, out_specs=(both, both, both), check_vma=False
    )
```
